32 devices in a mesh: dp: 4 (over y, core), gx: 4 (over z), gy: 2 (over x).
Axes of the slice: x: 2, y: 2, z: 4, core: 2. Of those that a mesh axis runs over, the one named last changes fastest.
Arguments:
- stream_in: bfloat16 [12288, 2048], P(('dp', 'gx'), 'gy'), may hold values from -11 to 11
- lengths: int32 [8], P('dp'), may hold values from 1024 to 1536, as said below
- routes: int32 [12288, 4], P('dp'), may hold values from 0 to 15, all different within a row; in each aligned block of 3072 rows (0 to 3071, 3072 to 6143, ...) at most 1152 rows name the same one
- route_weights: float32 [12288, 4], P('dp'), may hold values from 0.15 to 0.6
- norm_attn: bfloat16 [2048], P('gy'), may hold values from 0.5 to 1.5
- w_qkv: bfloat16 [2048, 16, 384], P('gy', 'gx'), may hold values from -0.125 to 0.125
- qkv_bias: bfloat16 [16, 384], P('gx'), may hold values from -1 to 1
- w_out: bfloat16 [2048, 2048], P('gx', 'gy'), may hold values from -1 to 1
- norm_ffn: bfloat16 [2048], P('gy'), may hold values from 0.5 to 1.5
- w_gate: bfloat16 [16, 2048, 1408], P(None, 'gy', 'gx'), may hold values from -0.125 to 0.125
- w_up: bfloat16 [16, 2048, 1408], P(None, 'gy', 'gx'), may hold values from -0.125 to 0.125
- w_down: bfloat16 [16, 1408, 2048], P(None, 'gx', 'gy'), may hold values from -0.15625 to 0.15625
- shared_gate: bfloat16 [2048, 5632], P('gy', 'gx'), may hold values from -0.125 to 0.125
- shared_up: bfloat16 [2048, 5632], P('gy', 'gx'), may hold values from -0.125 to 0.125
- shared_down: bfloat16 [5632, 2048], P('gx', 'gy'), may hold values from -0.078125 to 0.078125
- shared_router: bfloat16 [2048], P('gy'), may hold values from -0.125 to 0.125
- cotangent: bfloat16 [12288, 2048], P(('dp', 'gx'), 'gy'), may hold values from -6 to 6
Outputs:
- layer_out: bfloat16 [12288, 2048], P(('dp', 'gx'), 'gy')
- grad_stream: float32 [12288, 2048], P(('dp', 'gx'), 'gy')
- grad_norm_attn: float32 [2048], P('gy')
- grad_w_qkv: float32 [2048, 16, 384], P('gy', 'gx')
- grad_qkv_bias: float32 [16, 384], P('gx')
- grad_w_out: float32 [2048, 2048], P('gx', 'gy')
- grad_norm_ffn: float32 [2048], P('gy')
- grad_w_gate: float32 [16, 2048, 1408], P(None, 'gy', 'gx')
- grad_w_up: float32 [16, 2048, 1408], P(None, 'gy', 'gx')
- grad_w_down: float32 [16, 1408, 2048], P(None, 'gx', 'gy')
- grad_shared_gate: float32 [2048, 5632], P('gy', 'gx')
- grad_shared_up: float32 [2048, 5632], P('gy', 'gx')
- grad_shared_down: float32 [5632, 2048], P('gx', 'gy')
- grad_shared_router: float32 [2048], P('gy')
- rms_stats: float32 [4], replicated
The draws below stay inside these ranges and needn't reach their ends.
Inputs may be any that keep to these rules, and one draw needn't show every extreme that they name: `lengths`: entries of one group are in slot order; in every group one sequence has exactly 1536 tokens and another exactly 1024, the others lie between; the group's slots after its last sequence are padding. `routes`: each row names 4 different experts; within the 3072 rows of one group no expert is named more than 1152 times.
All inputs are finite; a program needn't handle non-finite values.
Results may differ from the reference program's by a relative error of at most 0.017.
The reference program's roundings to bfloat16 on the way count: a program that leaves them out, or rounds other values in their place, can miss the bound.
Values may be sent and summed in bfloat16 or wider, within the bound.
A program may use at most 704 MiB of HBM per device.

```python
import math
import jax
import jax.numpy as jnp
import numpy as np
from jax import lax

D = 2048
NH = 16
HD = 128
FE = 1408
FS = 5632
TOPK = 4
E = 16
LMIN = 1024
NSEQ = 2
LMAX = 1536
SLOTS = 3072
CAPACITY = 1152
SEQS = 8
TOKENS = 12288


def draw_stream_in(key, part):
    groups = TOKENS // SLOTS
    group_of = (jnp.arange(TOKENS, dtype=jnp.int32) // SLOTS).astype(jnp.float32)
    level = 0.6 * 3.0 ** (group_of / max(groups - 1, 1))
    base = jnp.clip(jax.random.normal(jax.random.fold_in(key, 21), (TOKENS, D), jnp.float32), -6.0, 6.0)
    return (base * level[:, None]).astype(jnp.bfloat16)


def draw_lengths(key, part):
    groups = SEQS // NSEQ
    base_draw = jax.random.randint(jax.random.fold_in(key, 11), (groups, NSEQ), LMIN, LMAX + 1)
    longest = jax.random.randint(jax.random.fold_in(key, 12), (groups, 1), 0, NSEQ)
    shortest = (longest + 1) % NSEQ
    columns = jnp.arange(NSEQ)[None, :]
    filled = jnp.where(columns == shortest, LMIN, base_draw)
    filled = jnp.where(columns == longest, LMAX, filled)
    return filled.reshape(groups * NSEQ).astype(jnp.int32)


def level_of(rng, extent, shards, smallest, top_value):
    level = 1.0
    for dim, blocks in shards:
        draws = jax.random.uniform(jax.random.fold_in(jax.random.fold_in(rng, 6), dim), (blocks,), jnp.float32, smallest / len(shards), top_value / len(shards))
        level = level * jnp.repeat(jnp.exp(draws), extent[dim] // blocks).reshape((-1,) + (1,) * (len(extent) - 1 - dim))
    return level


def deal_out(key, own, number, rows, amount, top, bound, slope):
    sequence = jax.random.permutation(key, amount)
    crowded, usual = portions_of(amount, rows * top, bound, slope, True), portions_of(amount, rows * top, bound, slope, False)
    places = jnp.arange(amount)

    def named(sizes, turn):
        used = int((sizes > 0).sum())
        fixed = max(1, used // 4)
        passed = fixed + (places - fixed + turn * (used - fixed)) % max(1, amount - fixed)
        return jnp.zeros((amount,), jnp.int32).at[sequence[jnp.where(places < fixed, places, passed)]].set(jnp.asarray(sizes, jnp.int32))

    sizes = jnp.where(number % 4 == 0, named(crowded, number // 4), named(usual, number - number // 4 - 1))
    mixed = jax.random.permutation(jax.random.fold_in(own, 3), amount)
    source_of, sink = mixed[0:amount // 2 * 2:2], mixed[1:amount // 2 * 2:2]
    margin = jnp.minimum(sizes[source_of] - 1, bound - sizes[sink]) // 2
    margin = jnp.where((source_of == sequence[0]) | (sink == sequence[0]) | (sizes[sink] == 0), 0, jnp.maximum(margin, 0))
    passed = jax.random.randint(jax.random.fold_in(own, 4), (amount // 2,), 0, 1 << 20) % (margin + 1)
    sizes = sizes.at[source_of].add(-passed).at[sink].add(passed)
    labels = jnp.searchsorted(jnp.cumsum(sizes), jnp.arange(rows * top), side="right").astype(jnp.int32)
    listing = labels.reshape(top, rows).T
    listing = listing[jax.random.permutation(jax.random.fold_in(own, 1), rows)]
    turn = jax.random.randint(jax.random.fold_in(own, 2), (rows, 1), 0, top)
    return jnp.take_along_axis(listing, (jnp.arange(top)[None, :] + turn) % top, axis=1)


def portions_of(amount, total, bound, lean, full):
    portions = [(1 << 20) // math.isqrt(rank ** lean) + 1 for rank in range(1, amount + 1)]
    largest = bound if full else min(bound, max(-(-total // amount), total * portions[0] // sum(portions)))
    least = 1 if total - largest >= amount - 1 else 0
    holding, surplus = [largest] + [least] * (amount - 1), total - largest - least * (amount - 1)
    while surplus > 0:
        free = [i for i in range(1, amount) if holding[i] < largest] or [i for i in range(1, amount) if holding[i] < bound]
        mass, remaining = sum([portions[i] for i in free]), surplus
        for i in free:
            addition = min(bound - holding[i], max(1, remaining * portions[i] // mass), surplus)
            holding[i] = holding[i] + addition
            surplus = surplus - addition
    return np.array(holding)


def centred(own_key, shape, deviation, reach, shards=(), kind=jnp.bfloat16):
    entries = jax.random.normal(own_key, shape, jnp.float32) * deviation
    if len(shards) > 0:
        entries = level_of(own_key, shape, shards, -0.22, 0.18) * entries
    return jnp.clip(entries, min=-reach, max=reach).astype(kind)


def setup_inputs(seed: int = 0) -> dict:
    seeds = jax.random.split(jax.random.key(seed), 18)
    stream_in = draw_stream_in(jax.random.fold_in(seeds[17], 71), 0)
    lengths = draw_lengths(jax.random.fold_in(seeds[17], 71), 0)
    routes_keys = jax.random.split(jax.random.fold_in(seeds[2], 1), TOKENS // SLOTS)
    routes_turns = jax.random.permutation(jax.random.fold_in(seeds[2], 3), TOKENS // SLOTS)
    routes = jax.vmap(lambda own, number: deal_out(jax.random.fold_in(seeds[2], 2), own, number, SLOTS, E, TOPK, CAPACITY, 1))(routes_keys, routes_turns).reshape((TOKENS, TOPK))
    route_weights = jnp.clip(0.15 + 0.45000002 * jax.random.uniform(seeds[3], (TOKENS, TOPK), jnp.float32) ** level_of(seeds[3], (TOKENS, TOPK), ((0, 4),), -0.2, 0.2), 0.15, 0.6)
    norm_attn = jnp.clip(1.0 + 0.1 * jax.random.normal(seeds[4], (D,), jnp.float32), 0.5, 1.5).astype(jnp.bfloat16)
    w_qkv = centred(seeds[5], (D, NH, 3 * HD), D ** -0.5, 0.125, ((0, 2), (1, 4)))
    qkv_bias = centred(seeds[6], (NH, 3 * HD), 0.15, 1.0, ((0, 4),))
    w_out = centred(seeds[7], (NH * HD, D), (HD // 4) ** -0.5, 1.0, ((0, 4), (1, 2)))
    norm_ffn = jnp.clip(1.0 + 0.1 * jax.random.normal(seeds[8], (D,), jnp.float32), 0.5, 1.5).astype(jnp.bfloat16)
    w_gate = centred(seeds[9], (E, D, FE), D ** -0.5, 0.125, ((1, 2), (2, 4)))
    w_up = centred(seeds[10], (E, D, FE), D ** -0.5, 0.125, ((1, 2), (2, 4)))
    w_down = centred(seeds[11], (E, FE, D), FE ** -0.5, 0.15625, ((1, 4), (2, 2)))
    shared_gate = centred(seeds[12], (D, FS), D ** -0.5, 0.125, ((0, 2), (1, 4)))
    shared_up = centred(seeds[13], (D, FS), D ** -0.5, 0.125, ((0, 2), (1, 4)))
    shared_down = centred(seeds[14], (FS, D), FS ** -0.5, 0.078125, ((0, 4), (1, 2)))
    shared_router = centred(seeds[15], (D,), D ** -0.5, 0.125, ((0, 2),))
    cotangent = centred(seeds[16], (TOKENS, D), 1.0, 6.0, ((0, 16), (1, 2)))
    return dict(stream_in=stream_in, lengths=lengths, routes=routes, route_weights=route_weights, norm_attn=norm_attn, w_qkv=w_qkv, qkv_bias=qkv_bias, w_out=w_out, norm_ffn=norm_ffn, w_gate=w_gate, w_up=w_up, w_down=w_down, shared_gate=shared_gate, shared_up=shared_up, shared_down=shared_down, shared_router=shared_router, cotangent=cotangent)


EPS = 1e-06
THETA = 1000000.0
NEG = -1e+30

@jax.custom_vjp
def low(v):
    return lax.optimization_barrier(v.astype(jnp.bfloat16)).astype(jnp.float32)

@jax.custom_vjp
def low_back(v):
    return v

def low_keep(v):
    return (low(v), None)

def low_pass(kept, grad):
    return (grad,)

def back_keep(v):
    return (v, None)

def back_low(kept, grad):
    return (low(grad),)
low.defvjp(low_keep, low_pass)
low_back.defvjp(back_keep, back_low)

def layout(length_group, slot_count):
    places = jnp.arange(slot_count, dtype=jnp.int32)
    seq_ends = jnp.cumsum(length_group).astype(jnp.int32)
    segment = lax.optimization_barrier(jnp.sum((places[:, None] >= seq_ends[None, :]).astype(jnp.int32), axis=1))
    starts = jnp.concatenate([jnp.zeros((1,), jnp.int32), seq_ends])
    seg_count = starts.shape[0]
    seq_begin = lax.optimization_barrier(jnp.sum(jnp.where(segment[:, None] == jnp.arange(seg_count, dtype=jnp.int32)[None, :], starts[None, :], 0), axis=1))
    return (segment, places - seq_begin, segment < length_group.shape[0])

def rotary_tables(positions, head_dim):
    half_dim = head_dim // 2
    frequency = THETA ** (-jnp.arange(half_dim, dtype=jnp.float32) * 2.0 / head_dim)
    angles = positions.astype(jnp.float32)[:, None] * frequency[None, :]
    return (jnp.cos(angles), jnp.sin(angles))

def rotate(values, cos_table, sin_table):
    half_dim = values.shape[-1] // 2
    front_half, back_half = (values[..., :half_dim], values[..., half_dim:])
    cosine, sine_part = (cos_table[:, None, :], sin_table[:, None, :])
    return jnp.concatenate([front_half * cosine - back_half * sine_part, back_half * cosine + front_half * sine_part], axis=-1)

def dispatch(route_group, weight_group, experts, capacity):
    flat_routes = route_group.reshape(-1).astype(jnp.int32)
    onehot = (flat_routes[:, None] == jnp.arange(experts, dtype=jnp.int32)[None, :]).astype(jnp.int32)
    rank_in = lax.optimization_barrier(jnp.sum(onehot * (jnp.cumsum(onehot, axis=0) - 1), axis=1))
    slot_of = (flat_routes * capacity + rank_in).astype(jnp.int32)
    owners = (jnp.arange(flat_routes.shape[0], dtype=jnp.int32) // route_group.shape[1]).astype(jnp.int32)
    slot_token = jnp.zeros((experts * capacity,), jnp.int32).at[slot_of].set(owners)
    slot_weight = jnp.zeros((experts * capacity,), jnp.float32).at[slot_of].set(weight_group.reshape(-1))
    slot_used = jnp.zeros((experts * capacity,), jnp.float32).at[slot_of].set(1.0)
    return (slot_of, slot_token, slot_weight, slot_used)

def group_forward(stream_group, length_group, route_group, weight_group, float_weights):
    norm_attn, w_qkv, qkv_bias, w_out, norm_ffn, w_gate, w_up, w_down, shared_gate, shared_up, shared_down, shared_router = float_weights
    highest = lax.Precision.HIGHEST
    segment, positions, valid_rows = layout(length_group, SLOTS)
    places = jnp.arange(SLOTS, dtype=jnp.int32)
    inv_attn = lax.rsqrt(lax.optimization_barrier(jnp.mean(stream_group * stream_group, axis=1, keepdims=True)) + EPS)
    normed = low(stream_group * inv_attn * norm_attn)
    mixed_rows = low_back(jnp.einsum('td,dhc->thc', normed, w_qkv, precision=highest) + qkv_bias)
    cos_table, sin_table = rotary_tables(positions, HD)
    queries = low(rotate(mixed_rows[..., :HD], cos_table, sin_table))
    key_rows = low(rotate(mixed_rows[..., HD:2 * HD], cos_table, sin_table))
    value_rows = low(mixed_rows[..., 2 * HD:])
    allowed = (segment[:, None] == segment[None, :]) & (places[None, :] <= places[:, None])
    score_scale = HD ** (-0.5)

    def one_head(head_in):
        query_head, key_head, value_head = head_in
        scores = low_back(jnp.dot(query_head, key_head.T, precision=highest) * score_scale)
        prob_rows = jax.nn.softmax(jnp.where(allowed, scores, NEG), axis=-1)
        return low_back(low(jnp.dot(low(prob_rows), value_head, precision=highest)))
    heads_out = lax.map(jax.checkpoint(one_head), (jnp.transpose(queries, (1, 0, 2)), jnp.transpose(key_rows, (1, 0, 2)), jnp.transpose(value_rows, (1, 0, 2))))
    attended = jnp.transpose(heads_out, (1, 0, 2)).reshape(SLOTS, NH * HD)
    attn_out = low_back(jnp.dot(attended, w_out, precision=highest))
    middle = stream_group + attn_out
    inv_ffn = lax.rsqrt(lax.optimization_barrier(jnp.mean(middle * middle, axis=1, keepdims=True)) + EPS)
    normed_ffn = low(middle * inv_ffn * norm_ffn)
    slot_of, slot_token, slot_weight, slot_used = dispatch(route_group, weight_group, E, CAPACITY)
    gathered = (normed_ffn[slot_token] * slot_used[:, None]).reshape(E, CAPACITY, D)
    gate_value = low_back(jnp.einsum('ecd,edf->ecf', gathered, w_gate, precision=highest))
    up_value = low_back(jnp.einsum('ecd,edf->ecf', gathered, w_up, precision=highest))
    hidden = low(jax.nn.silu(gate_value) * up_value)
    expert_out = low_back(jnp.einsum('ecf,efd->ecd', hidden, w_down, precision=highest)).reshape(E * CAPACITY, D)
    routed = lax.optimization_barrier(jnp.sum(expert_out[slot_of].reshape(SLOTS, TOPK, D) * weight_group[:, :, None], axis=1))
    sgate_value = low_back(jnp.dot(normed_ffn, shared_gate, precision=highest))
    sup_value = low_back(jnp.dot(normed_ffn, shared_up, precision=highest))
    gate_logit = jnp.dot(normed_ffn, shared_router, precision=highest)
    shared_hidden = low(jax.nn.sigmoid(gate_logit)[:, None] * jax.nn.silu(sgate_value) * sup_value)
    branch = routed + jnp.dot(shared_hidden, shared_down, precision=highest)
    result = middle + branch
    valid_mask = valid_rows.astype(jnp.float32)[:, None]
    square_sums = jnp.stack([jnp.sum(valid_mask * middle * middle), jnp.sum(valid_mask * result * result), jnp.sum(valid_mask * attn_out * attn_out), jnp.sum(valid_mask * branch * branch), jnp.sum(valid_rows.astype(jnp.float32)) * D])
    return (result, square_sums)

def reference(stream_in, lengths, routes, route_weights, norm_attn, w_qkv, qkv_bias, w_out, norm_ffn, w_gate, w_up, w_down, shared_gate, shared_up, shared_down, shared_router, cotangent):
    groups = lengths.shape[0] // NSEQ
    float_weights = tuple((weight_arg.astype(jnp.float32) for weight_arg in (norm_attn, w_qkv, qkv_bias, w_out, norm_ffn, w_gate, w_up, w_down, shared_gate, shared_up, shared_down, shared_router)))
    length_rows = lengths.reshape(groups, NSEQ)
    route_rows = routes.reshape(groups, SLOTS, TOPK)
    weight_rows = route_weights.astype(jnp.float32).reshape(groups, SLOTS, TOPK)

    def forward(stream_all, *weights_all):

        def group_step(totals, batch_in):
            stream_group, length_group, route_group, weight_group = batch_in
            result, square_sums = jax.checkpoint(group_forward)(stream_group, length_group, route_group, weight_group, weights_all)
            return (totals + square_sums, result)
        totals, outputs = lax.scan(group_step, jnp.zeros((5,), jnp.float32), (stream_all, length_rows, route_rows, weight_rows))
        return (outputs, totals)
    stream_all = stream_in.astype(jnp.float32).reshape(groups, SLOTS, D)
    (outputs, totals), pullback = jax.vjp(forward, stream_all, *float_weights)
    valid_all = lax.map(lambda length_group: layout(length_group, SLOTS)[2], length_rows)
    masked = cotangent.astype(jnp.float32).reshape(groups, SLOTS, D) * valid_all.astype(jnp.float32)[:, :, None]
    gradients = pullback((masked, jnp.zeros((5,), jnp.float32)))
    rms_stats = jnp.sqrt(totals[:4] / totals[4])
    return (outputs.reshape(groups * SLOTS, D).astype(jnp.bfloat16), gradients[0].reshape(groups * SLOTS, D), gradients[1], gradients[2], gradients[3], gradients[4], gradients[5], gradients[6], gradients[7], gradients[8], gradients[9], gradients[10], gradients[11], gradients[12], rms_stats)
```

```python
import functools

import jax
import jax.numpy as jnp
from jax import lax
from jax.experimental import pallas as pl
from jax.experimental.pallas import tpu as pltpu
from jax.sharding import PartitionSpec as P

HD = 128
E = 16
TM = 256
PIECE = 16
PAIR = 2

EPS = 1e-06
THETA = 1000000.0
NEG = -1e30
LOW = -1e20
LOG2E = 1.4426950408889634
F32 = jnp.float32
BF16 = jnp.bfloat16
LIMIT = 60 * 2**20


def dot(a, b, dims=((1,), (0,))):
    return lax.dot_general(a, b, (dims, ((), ())), preferred_element_type=F32)


def params(n=1):
    return pltpu.CompilerParams(
        dimension_semantics=("arbitrary",) * n, vmem_limit_bytes=LIMIT
    )


def cost(flops, nbytes):
    return pl.CostEstimate(flops=int(flops), bytes_accessed=int(nbytes), transcendentals=0)


def fixed(shape):
    zeros = (0,) * len(shape)
    return pl.BlockSpec(shape, lambda *_: zeros, pipeline_mode=pl.Buffered(1))


def turn(values, cos, sin):
    return values * cos + pltpu.roll(values, HD // 2, 1) * sin


def qkv_body(n1, w, bias, cos, sin, q_out, kv_out):
    mixed = dot(n1[...], w[...]) + bias[0].astype(F32)
    q_out[...] = turn(mixed[:, :HD], cos[...], sin[...]).astype(BF16)
    kv_out[:, :HD] = turn(mixed[:, HD : 2 * HD], cos[...], sin[...]).astype(BF16)
    kv_out[:, HD:] = mixed[:, 2 * HD :].astype(BF16)


def project_qkv(n1, w, bias, cos, sin):
    rows, depth = n1.shape
    heads = bias.shape[0]
    return pl.pallas_call(
        qkv_body,
        grid=(heads,),
        in_specs=[
            fixed((rows, depth)),
            pl.BlockSpec((depth, 3 * HD), lambda h: (0, h)),
            pl.BlockSpec((1, 1, 3 * HD), lambda h: (h, 0, 0)),
            fixed((rows, HD)),
            fixed((rows, HD)),
        ],
        out_specs=[
            pl.BlockSpec((rows, HD), lambda h: (0, h)),
            pl.BlockSpec((rows, 2 * HD), lambda h: (0, h)),
        ],
        out_shape=[
            jax.ShapeDtypeStruct((rows, heads * HD), BF16),
            jax.ShapeDtypeStruct((rows, heads * 2 * HD), BF16),
        ],
        compiler_params=params(),
        cost_estimate=cost(2 * rows * depth * heads * 3 * HD, 4 * rows * depth),
        name="project_qkv",
    )(n1, w, bias[:, None, :], cos, sin)


def first_of(place, ends, count):
    start = jnp.zeros_like(place)
    for n in range(count):
        start = jnp.where(place >= ends[n], ends[n], start)
    return start


def pair_visible(q_start, k_start, size, ends, count):
    begin = jnp.int32(0)
    for n in range(count):
        begin = jnp.where(q_start >= ends[n], ends[n], begin)
    return (k_start <= q_start + size - 1) & (k_start + size - 1 >= begin)


def allowed_mask(q_start, k_start, size, ends, count):
    q_place = q_start + lax.broadcasted_iota(jnp.int32, (size, 1), 0)
    k_place = k_start + lax.broadcasted_iota(jnp.int32, (1, size), 1)
    return (k_place <= q_place) & (k_place >= first_of(q_place, ends, count))


def attend_body(dims, meta, q, kv_own, kv_rem, o_out, exact_out, lse_out, top, main, extra):
    size, blocks, parts, count, pair = dims
    scale = HD ** (-0.5) * LOG2E
    j = pl.program_id(1)
    part = meta[count]
    span = size * parts
    ones = jnp.ones((size, HD), BF16)
    q_start = j * span + part * size
    top[...] = jnp.full_like(top, LOW)
    main[...] = jnp.zeros_like(main)
    extra[...] = jnp.zeros_like(extra)
    q_place = q_start + lax.broadcasted_iota(jnp.int32, (size, 1), 0)
    begin = first_of(q_place, meta, count)
    for shift in range(parts):
        owner = lax.rem(part + shift, parts)

        @pl.loop(0, j + 1)
        def _(jj):
            k_start = jj * span + owner * size

            @pl.when(pair_visible(q_start, k_start, size, meta, count))
            def _():
                if shift == 0:
                    there, kv = pl.ds(jj * size, size), kv_own
                else:
                    there, kv = pl.ds(((shift - 1) * blocks + jj) * size, size), kv_rem
                k_place = k_start + lax.broadcasted_iota(jnp.int32, (1, size), 1)
                allowed = (k_place <= q_place) & (k_place >= begin)
                for u in range(pair):
                    keys = kv[there, 2 * u * HD : (2 * u + 1) * HD]
                    values = kv[there, (2 * u + 1) * HD : (2 * u + 2) * HD]
                    s = dot(q[:, u * HD : (u + 1) * HD], keys, ((1,), (1,))) * scale
                    s = jnp.where(allowed, s, NEG)
                    old = top[u]
                    new = jnp.maximum(old, jnp.max(s, axis=1, keepdims=True))
                    p = jnp.exp2(s - new[:, :1])
                    fade = jnp.exp2(old - new)
                    fade = jnp.concatenate([fade, fade], axis=1)
                    coarse = p.astype(BF16)
                    fine = (p - coarse.astype(F32)).astype(BF16)
                    values = jnp.concatenate([values, ones], axis=1)
                    main[u] = main[u] * fade + dot(coarse, values)
                    extra[u] = extra[u] * fade + dot(fine, values)
                    top[u] = new

    for u in range(pair):
        here = slice(u * HD, (u + 1) * HD)
        exact = main[u] + extra[u]
        share = 1.0 / exact[:, HD:]
        o_out[:, here] = (main[u, :, :HD] * share).astype(BF16)
        exact_out[:, here] = exact[:, :HD] * share
        lse_out[:, here] = top[u] + jnp.log2(exact[:, HD:])


def attend(meta, q, kv_own, kv_rem, size, parts, count):
    rows, width = q.shape
    heads, blocks = width // HD, rows // size
    pair = next(n for n in (PAIR, 2, 1) if heads % n == 0)
    block = pl.BlockSpec((size, pair * HD), lambda h, j, *_: (j, h))
    return pl.pallas_call(
        functools.partial(attend_body, (size, blocks, parts, count, pair)),
        grid_spec=pltpu.PrefetchScalarGridSpec(
            num_scalar_prefetch=1,
            grid=(heads // pair, blocks),
            in_specs=[
                block,
                pl.BlockSpec((rows, 2 * pair * HD), lambda h, j, *_: (0, h)),
                pl.BlockSpec((rows * (parts - 1), 2 * pair * HD), lambda h, j, *_: (0, h)),
            ],
            out_specs=[block, block, block],
            scratch_shapes=[
                pltpu.VMEM((pair, size, HD), F32),
                pltpu.VMEM((pair, size, 2 * HD), F32),
                pltpu.VMEM((pair, size, 2 * HD), F32),
            ],
        ),
        out_shape=[
            jax.ShapeDtypeStruct((rows, width), BF16),
            jax.ShapeDtypeStruct((rows, width), F32),
            jax.ShapeDtypeStruct((rows, width), F32),
        ],
        compiler_params=params(2),
        cost_estimate=cost(12 * rows * rows * width, 30 * rows * width),
        name="attend",
    )(meta, q, kv_own, kv_rem)


def attend_back_body(
    dims, meta, q, kv_own, kv_rem, d_o, exact, lse, cos, sin, dq_out, own_out, rem_out, dq_sum, kv_sum
):
    size, blocks, parts, count = dims
    scale = HD ** (-0.5)
    part = meta[count]
    span = size * parts
    kv_sum[...] = jnp.zeros_like(kv_sum)

    @pl.loop(0, blocks)
    def _(j):
        q_start = j * span + part * size
        here = pl.ds(j * size, size)
        q_piece, do_piece = q[here, :], d_o[here, :]
        delta = jnp.sum(do_piece.astype(F32) * exact[here, :], axis=1, keepdims=True)
        level = lse[here, :][:, :1]
        dq_sum[...] = jnp.zeros_like(dq_sum)
        for shift in range(parts):
            owner = lax.rem(part + shift, parts)

            @pl.loop(0, j + 1)
            def _(jj):
                k_start = jj * span + owner * size

                @pl.when(pair_visible(q_start, k_start, size, meta, count))
                def _():
                    if shift == 0:
                        piece = kv_own[pl.ds(jj * size, size), :]
                    else:
                        piece = kv_rem[pl.ds(((shift - 1) * blocks + jj) * size, size), :]
                    there = pl.ds((shift * blocks + jj) * size, size)
                    allowed = allowed_mask(q_start, k_start, size, meta, count)
                    s = dot(q_piece, piece[:, :HD], ((1,), (1,))) * (scale * LOG2E)
                    p = jnp.where(allowed, jnp.exp2(s - level), 0.0)
                    dp = dot(do_piece, piece[:, HD:], ((1,), (1,)))
                    ds = (p * (dp - delta)).astype(BF16)
                    dq_sum[...] += dot(ds, piece[:, :HD])
                    kv_sum[there, :HD] += dot(ds, q_piece, ((0,), (0,)))
                    kv_sum[there, HD:] += dot(p.astype(BF16), do_piece, ((0,), (0,)))

        dq_out[here, :] = turn(dq_sum[...] * scale, cos[here, :], -sin[here, :]).astype(BF16)

    rows = blocks * size
    own_out[:, :HD] = kv_sum[:rows, :HD] * scale
    own_out[:, HD:] = kv_sum[:rows, HD:]
    rem_out[:, :HD] = (kv_sum[rows:, :HD] * scale).astype(BF16)
    rem_out[:, HD:] = kv_sum[rows:, HD:].astype(BF16)


def attend_back(meta, q, kv_own, kv_rem, d_o, exact, lse, cos, sin, size, parts, count):
    rows, width = q.shape
    heads, blocks = width // HD, rows // size
    narrow = pl.BlockSpec((rows, HD), lambda h, *_: (0, h))
    wide = pl.BlockSpec((rows, 2 * HD), lambda h, *_: (0, h))
    rest = pl.BlockSpec((rows * (parts - 1), 2 * HD), lambda h, *_: (0, h))
    return pl.pallas_call(
        functools.partial(attend_back_body, (size, blocks, parts, count)),
        grid_spec=pltpu.PrefetchScalarGridSpec(
            num_scalar_prefetch=1,
            grid=(heads,),
            in_specs=[narrow, wide, rest, narrow, narrow, narrow, fixed((rows, HD)), fixed((rows, HD))],
            out_specs=[narrow, wide, rest],
            scratch_shapes=[
                pltpu.VMEM((size, HD), F32),
                pltpu.VMEM((rows * parts, 2 * HD), F32),
            ],
        ),
        out_shape=[
            jax.ShapeDtypeStruct((rows, width), BF16),
            jax.ShapeDtypeStruct((rows, 2 * width), F32),
            jax.ShapeDtypeStruct((rows * (parts - 1), 2 * width), BF16),
        ],
        compiler_params=params(),
        cost_estimate=cost(20 * rows * rows * width, 40 * rows * width),
        name="attend_back",
    )(meta, q, kv_own, kv_rem, d_o, exact, lse, cos, sin)


def mix_body(arrived, dq, own, *refs):
    got, (cos, sin, out, bias_out) = refs[:arrived], refs[arrived:]
    total = own[...]
    for piece in got:
        total = total + piece[...].astype(F32)
    out[:, :HD] = dq[...]
    out[:, HD : 2 * HD] = turn(total[:, :HD], cos[...], -sin[...]).astype(BF16)
    out[:, 2 * HD :] = total[:, HD:].astype(BF16)
    bias_out[0] = jnp.sum(out[...].astype(F32), axis=0, keepdims=True)


def mix_back(dq, own, got, cos, sin):
    rows, width = dq.shape
    heads = width // HD
    wide = pl.BlockSpec((rows, 2 * HD), lambda h: (0, h))
    return pl.pallas_call(
        functools.partial(mix_body, len(got)),
        grid=(heads,),
        in_specs=[pl.BlockSpec((rows, HD), lambda h: (0, h)), wide]
        + [wide] * len(got)
        + [fixed((rows, HD)), fixed((rows, HD))],
        out_specs=[
            pl.BlockSpec((rows, 3 * HD), lambda h: (0, h)),
            pl.BlockSpec((1, 1, 3 * HD), lambda h: (h, 0, 0)),
        ],
        out_shape=[
            jax.ShapeDtypeStruct((rows, heads * 3 * HD), BF16),
            jax.ShapeDtypeStruct((heads, 1, 3 * HD), F32),
        ],
        compiler_params=params(),
        cost_estimate=cost(rows * width * 20, rows * width * 20),
        name="mix_back",
    )(dq, own, *got, cos, sin)


def plan_tiles(route_rows, weight_rows, block):
    rows, top = route_rows.shape
    blocks = rows // block
    per_tile = TM // PIECE
    room = (top * block + E * (PIECE - 1)) // PIECE
    number = (top * rows + E * blocks * (PIECE - 1) + E * TM) // TM
    experts = jnp.arange(E, dtype=jnp.int32)
    steps = jnp.arange(blocks, dtype=jnp.int32)
    match = route_rows[:, :, None] == experts
    spread = jnp.any(match, axis=1).T.reshape(E, blocks, block)
    order = jnp.arange(block, dtype=jnp.int32)
    before = (order[:, None] < order[None, :]).astype(BF16)
    rank = jnp.einsum("ebt,tu->ebu", spread.astype(BF16), before, preferred_element_type=F32)
    held = (jnp.sum(spread.astype(jnp.int32), axis=2) + PIECE - 1) // PIECE
    lower = (experts[:, None] < experts[None, :]).astype(jnp.int32)
    start = jnp.sum(lower[:, :, None] * held[:, None, :], axis=0)
    ahead = jnp.sum(
        jnp.where(steps[:, None] < steps[None, :], held[:, :, None], 0), axis=1
    )
    load = jnp.sum(held, axis=1)
    tiles = jnp.maximum((load + per_tile - 1) // per_tile, 1)
    begin = jnp.sum(lower * tiles[:, None], axis=0)
    spot = (rank.astype(jnp.int32) + start[:, :, None] * PIECE).reshape(E, rows).T
    spot = jnp.sum(jnp.where(match, spot[:, None, :], 0), axis=2)
    piece = jnp.arange(room, dtype=jnp.int32)
    inside = (piece[None, None, :] >= start[:, :, None]) & (
        piece[None, None, :] < (start + held)[:, :, None]
    )
    where_to = (begin[:, None] * per_tile + ahead - start)[:, :, None] + piece[None, None, :]
    where_to = jnp.sum(jnp.where(inside, where_to, 0), axis=0)
    halves = []
    for half in range(2):
        low, high = half * E // 2, (half + 1) * E // 2
        room_of = (top * rows + (high - low) * (blocks * (PIECE - 1) + TM)) // TM
        turn_in = jnp.arange(room_of, dtype=jnp.int32)
        from_tile = jnp.sum(tiles[:low])
        total = jnp.sum(tiles[low:high])
        place = from_tile + jnp.minimum(turn_in, total - 1)
        expert = jnp.sum((place[:, None] >= (begin + tiles)[None, :]).astype(jnp.int32), axis=1)
        pick = (expert[:, None] == experts[None, :]).astype(jnp.int32)
        turn_of = place - jnp.sum(pick * begin[None, :], axis=1)
        active = turn_in < total
        last = active & (turn_of == jnp.sum(pick * tiles[None, :], axis=1) - 1)
        limit = jnp.sum(pick * load[None, :], axis=1) * PIECE - turn_of * TM
        inner = turn_of[:, None] * per_tile + jnp.arange(per_tile, dtype=jnp.int32)[None, :]
        ahead_of = jnp.sum(pick[:, :, None] * ahead[None], axis=1)[:, None, :]
        held_of = jnp.sum(pick[:, :, None] * held[None], axis=1)[:, None, :]
        start_of = jnp.sum(pick[:, :, None] * start[None], axis=1)[:, None, :]
        inner = inner[:, :, None]
        inside = (inner >= ahead_of) & (inner < ahead_of + held_of)
        source = inner - ahead_of + start_of + (steps * room)[None, None, :]
        source = jnp.sum(jnp.where(inside, source, 0), axis=2)
        meta = jnp.stack(
            [
                expert,
                place,
                active.astype(jnp.int32),
                (active & (turn_of == 0)).astype(jnp.int32),
                last.astype(jnp.int32),
                limit,
            ]
        )
        halves.append((meta, source))
    spot = spot.reshape(blocks, block, top)
    weight = weight_rows.reshape(blocks, block, top)
    return dict(
        halves=halves,
        number=number,
        get=where_to,
        room=room,
        column=spot,
        line=jnp.swapaxes(spot, 1, 2),
        weight=weight,
        line_weight=jnp.swapaxes(weight, 1, 2),
    )


def send_out_body(dims, line, *refs):
    top, chunk, scaled = dims
    weight = refs[0] if scaled else None
    values, out, held = refs[-3:]
    rows, block = out.shape[1], values.shape[1]
    held[...] = values[0]

    @pl.loop(0, rows // chunk)
    def _(c):
        ids = lax.broadcasted_iota(jnp.int32, (chunk, block), 0) + c * chunk
        chosen = jnp.zeros((chunk, block), F32)
        level = jnp.zeros((chunk, block), F32)
        for r in range(top):
            hit = ids == line[0, r : r + 1, :]
            chosen = jnp.where(hit, 1.0, chosen)
            if scaled:
                level = jnp.where(hit, weight[0, r : r + 1, :], level)
        value = dot(chosen.astype(BF16), held[...])
        if scaled:
            value = value * jnp.sum(level, axis=1, keepdims=True)
        out[0, pl.ds(pl.multiple_of(c * chunk, chunk), chunk), :] = value.astype(BF16)


def send_out(plan, values, scaled):
    blocks, block, depth = values.shape
    top = plan["column"].shape[2]
    rows = plan["room"] * PIECE
    chunk = rows
    line = pl.BlockSpec((1, top, block), lambda b: (b, 0, 0))
    extra = [plan["line_weight"]] if scaled else []
    return pl.pallas_call(
        functools.partial(send_out_body, (top, chunk, scaled)),
        grid=(blocks,),
        in_specs=[line] * (1 + len(extra)) + [pl.BlockSpec((1, block, depth), lambda b: (b, 0, 0))],
        out_specs=pl.BlockSpec((1, rows, depth), lambda b: (b, 0, 0)),
        scratch_shapes=[pltpu.VMEM((block, depth), BF16)],
        out_shape=jax.ShapeDtypeStruct((blocks, rows, depth), BF16),
        compiler_params=params(),
        cost_estimate=cost(2 * blocks * rows * block * depth, 4 * blocks * rows * depth),
        name="send_out",
    )(plan["line"], *extra, values).reshape(blocks * rows, depth)


def bring_back_body(dims, get, column, *refs):
    blocks, top, room, weighted = dims
    weight = refs[0] if weighted else None
    packed, out, buf, sem = refs[-4:]
    b = pl.program_id(0)
    slot = lax.rem(b, 2)
    rows, block = buf.shape[1], out.shape[1]

    def fetch(which, into):
        @pl.loop(0, room)
        def _(i):
            pltpu.make_async_copy(
                packed.at[pl.ds(pl.multiple_of(get[which, i] * PIECE, PIECE), PIECE)],
                buf.at[into, pl.ds(pl.multiple_of(i * PIECE, PIECE), PIECE)],
                sem.at[into],
            ).start()

    @pl.when(b == 0)
    def _():
        fetch(b, slot)

    @pl.when(b < blocks - 1)
    def _():
        fetch(b + 1, 1 - slot)

    ids = lax.broadcasted_iota(jnp.int32, (block, rows), 1)
    chosen = jnp.zeros((block, rows), F32)
    for r in range(top):
        level = weight[0, :, r : r + 1] if weighted else 1.0
        chosen = jnp.where(ids == column[0, :, r : r + 1], level, chosen)
    pltpu.make_async_copy(packed.at[pl.ds(0, rows)], buf.at[slot], sem.at[slot]).wait()
    out[0] = dot(chosen.astype(BF16), buf[slot]).astype(BF16)


def bring_back(plan, packed, block, weighted):
    blocks, room = plan["get"].shape
    top = plan["column"].shape[2]
    depth = packed.shape[1]
    rows = room * PIECE
    column = pl.BlockSpec((1, block, top), lambda b, *_: (b, 0, 0))
    extra = [plan["weight"]] if weighted else []
    return pl.pallas_call(
        functools.partial(bring_back_body, (blocks, top, room, weighted)),
        grid_spec=pltpu.PrefetchScalarGridSpec(
            num_scalar_prefetch=1,
            grid=(blocks,),
            in_specs=[column] * (1 + len(extra)) + [pl.BlockSpec(memory_space=pl.ANY)],
            out_specs=pl.BlockSpec((1, block, depth), lambda b, *_: (b, 0, 0)),
            scratch_shapes=[pltpu.VMEM((2, rows, depth), BF16), pltpu.SemaphoreType.DMA((2,))],
        ),
        out_shape=jax.ShapeDtypeStruct((blocks, block, depth), BF16),
        compiler_params=params(),
        cost_estimate=cost(2 * blocks * rows * block * depth, 4 * blocks * rows * depth),
        name="bring_back",
    )(plan["get"], plan["column"], *extra, packed)


def experts_body(dims, meta, source, spot, x, d, gu_own, gu_rem, down_own, down_rem, *refs):
    cut, number, hidden, later = dims
    got, refs = (refs[:4], refs[6:]) if later else ((), refs)
    out, dx = refs[:2]
    results = refs[2:6]
    xs, ds, dgu = refs[6:9]
    totals, sem = refs[9:13], refs[13]
    i = pl.program_id(0)
    slot = lax.rem(i, 2)
    rows, cols = ((0,), (0,)), ((1,), (1,))

    def fetch(which, into):
        @pl.loop(0, TM // PIECE)
        def _(n):
            there = pl.ds(pl.multiple_of(source[which, n] * PIECE, PIECE), PIECE)
            here = pl.ds(pl.multiple_of(n * PIECE, PIECE), PIECE)
            pltpu.make_async_copy(x.at[there], xs.at[into, here], sem.at[0, into]).start()
            pltpu.make_async_copy(d.at[there], ds.at[into, here], sem.at[1, into]).start()

    @pl.when(i == 0)
    def _():
        fetch(i, slot)

    @pl.when((i < number - 1) & (meta[2, jnp.minimum(i + 1, number - 1)] == 1))
    def _():
        fetch(i + 1, 1 - slot)

    @pl.when(meta[3, i] == 1)
    def _():
        for total in totals:
            total[...] = jnp.zeros_like(total)

    @pl.when(meta[2, i] == 1)
    def _():
        pltpu.make_async_copy(x.at[pl.ds(0, TM)], xs.at[slot], sem.at[0, slot]).wait()
        pltpu.make_async_copy(d.at[pl.ds(0, TM)], ds.at[slot], sem.at[1, slot]).wait()
        limit = meta[5, i]

        @pl.when(limit < TM)
        def _():
            inside = lax.broadcasted_iota(jnp.int32, xs.shape[1:], 0) < limit
            for ref in (xs, ds):
                ref[slot] = jnp.where(inside, ref[slot], jnp.zeros(xs.shape[1:], BF16))

        x_own, x_rem = xs[slot, :, :cut], xs[slot, :, cut:]
        d_own, d_rem = ds[slot, :, :cut], ds[slot, :, cut:]
        both = dot(x_own, gu_own[0], cols) + dot(x_rem, gu_rem[0], cols)
        gate, up = both[:, :hidden], both[:, hidden:]
        d_hidden = dot(d_own, down_own[0], cols) + dot(d_rem, down_rem[0], cols)
        logistic = jax.nn.sigmoid(gate)
        act = gate * logistic
        h = (act * up).astype(BF16)
        dgu[:, :hidden] = (d_hidden * up * logistic * (1.0 + gate * (1.0 - logistic))).astype(BF16)
        dgu[:, hidden:] = (d_hidden * act).astype(BF16)
        out[:, :cut] = dot(h, down_own[0]).astype(BF16)
        out[:, cut:] = dot(h, down_rem[0]).astype(BF16)
        dx[:, :cut] = dot(dgu[...], gu_own[0]).astype(BF16)
        dx[:, cut:] = dot(dgu[...], gu_rem[0]).astype(BF16)
        totals[0][...] += dot(dgu[...], x_own, rows)
        totals[1][...] += dot(dgu[...], x_rem, rows)
        totals[2][...] += dot(h, d_own, rows)
        totals[3][...] += dot(h, d_rem, rows)

    @pl.when(meta[4, i] == 1)
    def _():
        for n, (total, to) in enumerate(zip(totals, results)):
            if later:
                to[0] = (total[...] + got[n][0].astype(F32)).astype(BF16)
            else:
                to[0] = total[...].astype(BF16)


def experts(plan, half, spot, x, d, weights, copies, got=(), filled=()):
    meta, source = plan["halves"][half]
    depth = x.shape[1]
    hidden, cut = weights[2].shape[1:]
    rest = depth - cut
    number = meta.shape[1]
    quarter = E // copies
    own_at = lambda i, meta, source, spot: (meta[0, i] ^ spot[1], 0, 0)
    rem_at = lambda i, meta, source, spot: (
        (((meta[0, i] ^ spot[1]) // quarter) ^ spot[0]) * quarter + meta[0, i] % quarter,
        0,
        0,
    )
    half_at = lambda i, meta, *_: (meta[0, i] - half * (E // 2), 0, 0)
    tile = pl.BlockSpec((TM, depth), lambda i, meta, *_: (meta[1, i], 0))
    shapes = [(2 * hidden, cut), (2 * hidden, rest), (hidden, cut), (hidden, rest)]
    anywhere = pl.BlockSpec(memory_space=pl.ANY)
    results = [pl.BlockSpec((1,) + s, half_at) for s in shapes]
    return pl.pallas_call(
        functools.partial(experts_body, (cut, number, hidden, half == 1)),
        grid_spec=pltpu.PrefetchScalarGridSpec(
            num_scalar_prefetch=3,
            grid=(number,),
            in_specs=[anywhere] * 2
            + [pl.BlockSpec((1,) + s, at) for s, at in zip(shapes, (own_at, rem_at) * 2)]
            + (results + [anywhere] * 2 if half else []),
            out_specs=[tile, tile] + results,
            scratch_shapes=[pltpu.VMEM((2, TM, depth), BF16)] * 2
            + [pltpu.VMEM((TM, 2 * hidden), BF16)]
            + [pltpu.VMEM(s, F32) for s in shapes]
            + [pltpu.SemaphoreType.DMA((2, 2))],
        ),
        out_shape=[jax.ShapeDtypeStruct((plan["number"] * TM, depth), BF16)] * 2
        + [jax.ShapeDtypeStruct((E // 2,) + s, BF16) for s in shapes],
        input_output_aliases={13: 0, 14: 1} if half else {},
        compiler_params=params(),
        cost_estimate=cost(9 * plan["number"] * TM * depth * hidden, 6 * E * depth * hidden + number * TM * depth * 4),
        name=("experts_first", "experts_second")[half],
    )(meta, source, spot, x, d, *weights, *got, *filled)


def from_ahead(values, shift):
    n = lax.axis_size("gy")
    return lax.ppermute(values, "gy", [(s, (s - shift) % n) for s in range(n)])


def across(values, bit):
    n = lax.axis_size("dp")
    return lax.ppermute(values, "dp", [(d, d ^ bit) for d in range(n)])


def bits():
    n, bit, out = lax.axis_size("dp"), 1, []
    while bit < n:
        out.append(bit)
        bit *= 2
    return out


def tie(values, *others):
    return lax.optimization_barrier((values, others))[0]


class Spread:
    def __init__(self, weights):
        self.weights = weights

    def cut(self):
        copies, me = lax.axis_size("dp"), lax.axis_index("dp")
        return [
            lax.dynamic_slice_in_dim(w, me * (w.shape[0] // copies), w.shape[0] // copies)
            for w, _ in self.weights
        ]

    def over_gy(self, pieces):
        parts = lax.axis_size("gy")
        out = []
        for piece, (_, axis) in zip(pieces, self.weights):
            got = [from_ahead(piece, k) for k in range(1, parts)]
            out.append({0: got[0] if len(got) == 1 else jnp.concatenate(got, axis=axis)})
        return out

    def over_dp(self, held, level):
        bit = list(reversed(bits()))[level]
        return [h | {key | bit: across(part, bit) for key, part in h.items()} for h in held]


def keyed(held):
    return jnp.concatenate([held[key] for key in range(len(held))], axis=0)


def whole(weight, axis, held):
    me = lax.axis_index("dp")
    stack = [held[key] for key in range(len(held))]
    for bit in bits():
        swap = (me & bit) != 0
        stack = [jnp.where(swap, stack[n ^ bit], stack[n]) for n in range(len(stack))]
    return jnp.concatenate([weight, jnp.concatenate(stack, axis=0)], axis=axis)


def to_rows(values):
    parts, me = lax.axis_size("gy"), lax.axis_index("gy")
    share = values.shape[0] // parts
    take = lambda k: lax.dynamic_slice_in_dim(values, ((me - k + parts) % parts) * share, share)
    return jnp.concatenate(
        [take(0)] + [from_ahead(take(k), k) for k in range(1, parts)], axis=1
    )


def to_columns(values, kind):
    parts, me = lax.axis_size("gy"), lax.axis_index("gy")
    width = values.shape[1] // parts
    blocks = []
    for k in range(parts):
        block = values[:, k * width : (k + 1) * width]
        blocks.append((from_ahead(block.astype(BF16), parts - k) if k else block).astype(kind))
    return jnp.concatenate(in_order([blocks[(parts - k) % parts] for k in range(parts)], me), axis=0)


def in_order(blocks, me):
    n = len(blocks)
    out = []
    for place in range(n):
        block = blocks[place]
        for k in range(n):
            block = jnp.where(me == (place - k) % n, blocks[k], block)
        out.append(block)
    return out


class Reduce:
    def __init__(self):
        self.side = lax.axis_index("dp") & 1

    def pick(self, values, side):
        half = values.shape[0] // 2
        return lax.dynamic_slice_in_dim(values, side * half, half)

    def near(self, grads):
        sums = []
        for grad in grads:
            sums.append([])
            for v in grad:
                got = across(self.pick(v, 1 - self.side), 1)
                sums[-1].append((self.pick(v, self.side).astype(F32) + got.astype(F32)).astype(BF16))
        return sums

    def over_gy(self, sums):
        parts = lax.axis_size("gy")
        out = []
        for own, *rest in sums:
            total = own.astype(F32)
            for k, piece in enumerate(rest, start=1):
                total = total + from_ahead(piece, parts - k).astype(F32)
            out.append(total.astype(BF16))
        return out

    def over_dp(self, sums):
        for bit in bits()[1:]:
            sums = [(t.astype(F32) + across(t, bit).astype(F32)).astype(BF16) for t in sums]
        return sums

    def finish(self, sums):
        out = []
        for total in sums:
            other = across(total, 1)
            first = jnp.where(self.side == 0, total, other).astype(F32)
            second = jnp.where(self.side == 0, other, total).astype(F32)
            out.append(jnp.concatenate([first, second], axis=0))
        return out


def split_blocks(values, parts, axis):
    width = values.shape[axis] // parts
    return [lax.slice_in_dim(values, k * width, (k + 1) * width, axis=axis) for k in range(parts)]


def gather_rows(values):
    return lax.all_gather(values, "gx", axis=0, tiled=True)


def sum_rows(values):
    return lax.psum_scatter(values, "gx", scatter_dimension=0, tiled=True)


def local(
    stream_in, lengths, routes, route_weights, norm_attn, w_qkv, qkv_bias, w_out, norm_ffn, w_gate, w_up,
    w_down, shared_gate, shared_up, shared_down, shared_router, cotangent
):
    parts, gy = lax.axis_size("gy"), lax.axis_index("gy")
    groups, gx = lax.axis_size("gx"), lax.axis_index("gx")
    dp = lax.axis_index("dp")
    held, width = stream_in.shape
    depth = width * parts
    size = held // parts
    rows = size * groups
    heads = qkv_bias.shape[0]
    count = lengths.shape[0]

    numbers = jnp.arange(count)
    ends = jnp.sum(jnp.where(numbers[:, None] <= numbers[None, :], lengths[:, None], 0), axis=0)
    ends = ends.astype(jnp.int32)
    row = jnp.arange(rows, dtype=jnp.int32)
    place = (row // size) * held + gy * size + row % size
    begin = jnp.zeros_like(place)
    for n in range(count):
        begin = jnp.where(place >= ends[n], ends[n], begin)
    mine = gx * held + gy * size + jnp.arange(size, dtype=jnp.int32)
    valid = (mine < ends[count - 1]).astype(F32)[:, None]
    half = HD // 2
    angles = (place - begin).astype(F32)[:, None] * (
        THETA ** (-jnp.arange(half, dtype=F32) * 2.0 / HD)
    )[None, :]
    cos, sin = jnp.cos(angles), jnp.sin(angles)
    cos = jnp.concatenate([cos, cos], axis=1)
    sin = jnp.concatenate([-sin, sin], axis=1)
    span = jnp.concatenate([ends, gy[None].astype(jnp.int32)])

    narrow = jnp.concatenate([norm_attn[None], norm_ffn[None], shared_router[None]])
    stream_rows, dy_rows = to_rows(stream_in), to_rows(cotangent)
    narrow = jnp.concatenate([narrow] + [from_ahead(narrow, k) for k in range(1, parts)], axis=1)
    gain_attn, gain_ffn, router = (narrow[n].astype(F32)[None, :] for n in range(3))
    flat_qkv = w_qkv.reshape(width, heads * 3 * HD)
    lead = Spread([(flat_qkv, 0), (w_out, 1)])
    gate_t, up_t = jnp.swapaxes(w_gate, 1, 2), jnp.swapaxes(w_up, 1, 2)
    early = Spread([(shared_gate, 0), (shared_up, 0), (shared_down, 1), (gate_t, 2)])
    late = [Spread([(up_t, 2)]), Spread([(w_down, 2)])]

    stream = stream_rows.astype(F32)
    inv_attn = lax.rsqrt(jnp.mean(stream * stream, axis=1, keepdims=True) + EPS)
    unit_attn = stream * inv_attn
    n1_part = (unit_attn * gain_attn).astype(BF16)
    lead_held = lead.over_gy(tie(lead.cut(), stream_rows))
    masked = dy_rows.astype(F32) * valid
    dy_part = masked.astype(BF16)
    early_held = early.over_gy(tie(early.cut(), dy_rows))
    n1 = gather_rows(n1_part)
    lead_held = lead.over_dp(lead_held, 0)
    lead_held = lead.over_dp(lead_held, 1)
    qkv_all = whole(flat_qkv, 0, lead_held[0])
    out_all = whole(w_out, 1, lead_held[1])
    n1, dy_part, qkv_all, out_all = lax.optimization_barrier((n1, dy_part, qkv_all, out_all))
    dy = gather_rows(dy_part)

    q, kv = project_qkv(n1, qkv_all, qkv_bias, cos, sin)
    kv, early_held = lax.optimization_barrier((kv, early_held))
    kv_rest = [from_ahead(kv, k) for k in range(1, parts)]
    kv_rest = kv_rest[0] if parts == 2 else jnp.concatenate(kv_rest, axis=0)
    shared_held, gate_held = early_held[:3], early_held[3:]
    gate_held = early.over_dp(gate_held, 0)
    kv_rest, gate_held = lax.optimization_barrier((kv_rest, gate_held))
    shared_held = early.over_dp(shared_held, 0)
    up_held = late[0].over_gy(tie(late[0].cut(), kv_rest))
    o, o_exact, level = attend(span, q, kv, kv_rest, size, parts, count)
    o, up_held, shared_held = lax.optimization_barrier((o, up_held, shared_held))
    attn_part = dot(o, out_all).astype(BF16)
    attn_part, dy = lax.optimization_barrier((attn_part, dy))
    attn = sum_rows(attn_part).astype(F32)
    down_held = late[1].over_gy(tie(late[1].cut(), o))
    shared_held = early.over_dp(shared_held, 1)
    gate_held = early.over_dp(gate_held, 1)
    up_held = late[0].over_dp(up_held, 0)

    block = 256 if rows % 256 == 0 else 128
    shape = (rows // block, block, depth)
    take = lambda v: lax.dynamic_index_in_dim(
        v.reshape(groups, parts, size, v.shape[1]), gy, 1, keepdims=False
    ).reshape(rows, v.shape[1])
    flip = (1 - (dp & 1)) * (E // 2)
    plan = plan_tiles(take(routes) ^ flip, take(route_weights), block)
    spot = jnp.stack([dp, flip]).astype(jnp.int32)
    d_slots = send_out(plan, dy.reshape(shape), True)
    sg_all = whole(shared_gate, 0, shared_held[0])
    su_all = whole(shared_up, 0, shared_held[1])
    sd_all = whole(shared_down, 1, shared_held[2])
    cols, both = ((1,), (1,)), ((0,), (0,))
    d_s_hidden = dot(dy, sd_all, cols)

    middle = stream + attn
    inv_ffn = lax.rsqrt(jnp.mean(middle * middle, axis=1, keepdims=True) + EPS)
    unit_ffn = middle * inv_ffn
    n2_part = (unit_ffn * gain_ffn).astype(BF16)
    n2_part, up_held, down_held, d_slots, d_s_hidden, plan["halves"] = lax.optimization_barrier(
        (n2_part, up_held, down_held, d_slots, d_s_hidden, plan["halves"])
    )
    n2 = gather_rows(n2_part)
    up_held = late[0].over_dp(up_held, 1)
    down_held = late[1].over_dp(down_held, 0)
    down_held = late[1].over_dp(down_held, 1)
    copies = lax.axis_size("dp")
    weights = [
        jnp.concatenate([gate_t, up_t], axis=1),
        jnp.concatenate(
            [jnp.concatenate([gate_held[0][key], up_held[0][key]], axis=1) for key in range(copies)], axis=0
        ),
        w_down,
        keyed(down_held[0]),
    ]

    n2, weights = lax.optimization_barrier((n2, weights))
    x_slots = send_out(plan, n2.reshape(shape), False)
    out_slots, dx_slots, *given = experts(plan, 0, spot, x_slots, d_slots, weights, copies)

    n2_s = tie(n2, given)
    got = [across(v, 1) for v in given]
    logit = jnp.sum(n2_s.astype(F32) * router, axis=1, keepdims=True)
    mixer = jax.nn.sigmoid(logit)
    sgate, sup = dot(n2_s, sg_all), dot(n2_s, su_all)
    s_logistic = jax.nn.sigmoid(sgate)
    s_act = sgate * s_logistic
    s_hidden = (mixer * s_act * sup).astype(BF16)
    d_sgate = (d_s_hidden * mixer * sup * s_logistic * (1.0 + sgate * (1.0 - s_logistic))).astype(BF16)
    d_sup = (d_s_hidden * mixer * s_act).astype(BF16)
    d_logit = jnp.sum(d_s_hidden * s_act * sup, axis=1, keepdims=True) * mixer * (1.0 - mixer)
    pieces = [
        [dot(a, d_sgate, both).astype(BF16) for a in split_blocks(n2_s, parts, 1)],
        [dot(a, d_sup, both).astype(BF16) for a in split_blocks(n2_s, parts, 1)],
        [dot(s_hidden, a, both).astype(BF16) for a in split_blocks(dy, parts, 1)],
    ]
    reduce = Reduce()
    shared_sums = reduce.near(pieces)
    dn2_shared = (
        dot(d_sgate, sg_all, cols) + dot(d_sup, su_all, cols) + d_logit * router
    ).astype(BF16)

    x_slots, shared_sums, dn2_shared, got = lax.optimization_barrier(
        (x_slots, shared_sums, dn2_shared, got)
    )
    out_slots, dx_slots, *sums = experts(
        plan, 1, spot, x_slots, d_slots, weights, copies, got, (out_slots, dx_slots)
    )
    shared_sums = reduce.over_gy(shared_sums)
    dx_slots, out_slots, shared_sums, sums = lax.optimization_barrier(
        (dx_slots, out_slots, shared_sums, sums)
    )
    down_sums = [[sums[2]] + split_blocks(sums[3], parts - 1, 2)]
    cuts = (0, E // 4, 3 * E // 8, E // 2)
    gu_sums = [
        [[sums[0][low:high]] + split_blocks(sums[1][low:high], parts - 1, 2)]
        for low, high in zip(cuts, cuts[1:])
    ]
    dn2 = bring_back(plan, dx_slots, block, False)
    dn2 = (dn2.reshape(rows, depth).astype(F32) + dn2_shared.astype(F32)).astype(BF16)
    d_n2 = sum_rows(dn2).astype(F32)
    down_sums = reduce.over_gy(down_sums)
    shared_sums = reduce.over_dp(shared_sums)
    routed = bring_back(plan, tie(out_slots, dn2), block, True)
    branch_part = (routed.reshape(rows, depth).astype(F32) + dot(s_hidden, sd_all)).astype(BF16)
    router_part = jnp.sum(d_logit * n2_s.astype(F32), axis=0)

    gain_ffn_part = jnp.sum(d_n2 * unit_ffn, axis=0)
    scaled = d_n2 * gain_ffn
    d_middle = masked + inv_ffn * (
        scaled - unit_ffn * jnp.mean(scaled * unit_ffn, axis=1, keepdims=True)
    )

    d_mid_part = d_middle.astype(BF16)
    d_mid_part, down_sums, branch_part, shared_sums, gu_sums = lax.optimization_barrier(
        (d_mid_part, down_sums, branch_part, shared_sums, gu_sums)
    )
    d_mid = gather_rows(d_mid_part)
    gu_sums[0] = reduce.over_gy(gu_sums[0])
    down_sums = reduce.over_dp(down_sums)
    grad_sgate, grad_sup, grad_sdown = reduce.finish(shared_sums)
    d_mid, gu_sums, down_sums, branch_part = lax.optimization_barrier(
        (d_mid, gu_sums, down_sums, branch_part)
    )
    branch = sum_rows(branch_part).astype(F32)
    d_o = dot(d_mid, out_all, cols).astype(BF16)
    gu_sums[0] = reduce.over_dp(gu_sums[0])
    gu_sums[1] = reduce.over_gy(gu_sums[1])
    dq, dkv_own, dkv_rest = attend_back(
        span, q, kv, kv_rest, d_o, o_exact, level, cos, sin, size, parts, count
    )
    dkv_rest, gu_sums[1:] = lax.optimization_barrier((dkv_rest, gu_sums[1:]))
    out_sums = reduce.near([[dot(o, b, both).astype(BF16) for b in split_blocks(d_mid, parts, 1)]])
    got = [
        from_ahead(piece, parts - k)
        for k, piece in enumerate(split_blocks(dkv_rest, parts - 1, 0), start=1)
    ]
    [grad_down] = reduce.finish(down_sums)
    got, out_sums, gu_sums = lax.optimization_barrier((got, out_sums, gu_sums))
    gu_sums[1] = reduce.over_dp(gu_sums[1])
    gu_sums[2] = reduce.over_gy(gu_sums[2])
    d_mixed, bias_part = mix_back(dq, dkv_own, got, cos, sin)
    d_n1_part = dot(d_mixed, qkv_all, cols).astype(BF16)
    d_n1 = sum_rows(d_n1_part).astype(F32)
    d_mixed = tie(d_mixed, d_n1_part)
    qkv_sums = reduce.near([[dot(a, d_mixed, both).astype(BF16) for a in split_blocks(n1, parts, 1)]])
    attn_sums = reduce.over_gy(qkv_sums + out_sums)
    gu_sums[2] = reduce.over_dp(gu_sums[2])
    grad_w_qkv, grad_w_out = reduce.finish(reduce.over_dp(attn_sums))
    grad_w_qkv = grad_w_qkv.reshape(width, heads, 3 * HD)
    result = middle + branch

    sums = jnp.stack([gain_ffn_part, router_part])
    sums = lax.dynamic_slice_in_dim(
        jnp.concatenate([sums, sums], axis=1), ((parts - gy) % parts) * width, depth, axis=1
    )
    flat_bias = bias_part.reshape(-1)
    biases = lax.dynamic_update_slice_in_dim(
        jnp.zeros((groups * flat_bias.shape[0],), F32), flat_bias, gx * flat_bias.shape[0], 0
    )
    squares = jnp.stack(
        [jnp.sum(valid * v * v) for v in (middle, result, attn, branch)] + [jnp.sum(valid) * depth]
    )
    sums = tie(jnp.concatenate([sums.reshape(-1), biases, squares]), d_n1_part)
    sums = lax.psum(sums, ("dp", "gx", "gy"))
    d_n1, sums = lax.optimization_barrier((d_n1, sums))
    hidden = gate_t.shape[1]
    gu = [gu_sum for [gu_sum] in gu_sums]
    gu_other = [across(v, 1) for v in gu]
    side = dp & 1
    grad_gate, grad_up = (
        jnp.swapaxes(
            jnp.concatenate(
                [jnp.where(side == 0, a[:, part], b[:, part]) for a, b in zip(gu, gu_other)]
                + [jnp.where(side == 0, b[:, part], a[:, part]) for a, b in zip(gu, gu_other)],
                axis=0,
            ).astype(F32),
            1,
            2,
        )
        for part in (slice(0, hidden), slice(hidden, 2 * hidden))
    )
    gain_attn_part = jnp.sum(d_n1 * unit_attn, axis=0)
    scaled = d_n1 * gain_attn
    grad_stream = d_middle + inv_attn * (
        scaled - unit_attn * jnp.mean(scaled * unit_attn, axis=1, keepdims=True)
    )

    def added(vectors):
        own, *rest = split_blocks(vectors, parts, 1)
        for k, piece in enumerate(rest, start=1):
            own = own + from_ahead(piece, parts - k)
        return jnp.sum(lax.all_gather(own, ("dp", "gx")), axis=0)

    [gain_sum] = added(gain_attn_part[None])
    vectors = lax.dynamic_slice_in_dim(sums[: 2 * depth].reshape(2, depth), gy * width, width, axis=1)
    bias_sum = lax.dynamic_slice_in_dim(sums[2 * depth : -5], gx * flat_bias.shape[0], flat_bias.shape[0])
    bias_sum = bias_sum.reshape(heads, 3 * HD)
    rms_stats = jnp.sqrt(sums[-5:-1] / sums[-1])
    return (
        to_columns(result, BF16),
        to_columns(grad_stream, F32),
        gain_sum,
        grad_w_qkv,
        bias_sum,
        grad_w_out,
        vectors[0],
        grad_gate,
        grad_up,
        grad_down,
        grad_sgate,
        grad_sup,
        grad_sdown,
        vectors[1],
        rms_stats,
    )


def solution(mesh):
    placed = (
        P(("dp", "gx"), "gy"),
        P("dp"),
        P("dp", None),
        P("dp", None),
        P("gy"),
        P("gy", "gx", None),
        P("gx", None),
        P("gx", "gy"),
        P("gy"),
        P(None, "gy", "gx"),
        P(None, "gy", "gx"),
        P(None, "gx", "gy"),
        P("gy", "gx"),
        P("gy", "gx"),
        P("gx", "gy"),
        P("gy"),
        P(("dp", "gx"), "gy"),
    )
    return jax.shard_map(
        local,
        mesh=mesh,
        in_specs=placed,
        out_specs=(
            P(("dp", "gx"), "gy"),
            P(("dp", "gx"), "gy"),
            P("gy"),
            P("gy", "gx", None),
            P("gx", None),
            P("gx", "gy"),
            P("gy"),
            P(None, "gy", "gx"),
            P(None, "gy", "gx"),
            P(None, "gx", "gy"),
            P("gy", "gx"),
            P("gy", "gx"),
            P("gx", "gy"),
            P("gy"),
            P(),
        ),
        check_vma=False,
    )
```

```python
import functools

import jax
import jax.numpy as jnp
from jax import lax
from jax.experimental import pallas as pl
from jax.experimental.pallas import tpu as pltpu
from jax.sharding import PartitionSpec as P

HD = 128
E = 16
TM = 256
PIECE = 16
PAIR = 2

EPS = 1e-06
THETA = 1000000.0
NEG = -1e30
LOW = -1e20
LOG2E = 1.4426950408889634
F32 = jnp.float32
BF16 = jnp.bfloat16
LIMIT = 60 * 2**20


def dot(a, b, dims=((1,), (0,))):
    return lax.dot_general(a, b, (dims, ((), ())), preferred_element_type=F32)


def params(n=1):
    return pltpu.CompilerParams(
        dimension_semantics=("arbitrary",) * n, vmem_limit_bytes=LIMIT
    )


def cost(flops, nbytes):
    return pl.CostEstimate(flops=int(flops), bytes_accessed=int(nbytes), transcendentals=0)


def fixed(shape):
    zeros = (0,) * len(shape)
    return pl.BlockSpec(shape, lambda *_: zeros, pipeline_mode=pl.Buffered(1))


def turn(values, cos, sin):
    return values * cos + pltpu.roll(values, HD // 2, 1) * sin


def qkv_body(n1, w, bias, cos, sin, q_out, kv_out):
    mixed = dot(n1[...], w[...]) + bias[0].astype(F32)
    q_out[...] = turn(mixed[:, :HD], cos[...], sin[...]).astype(BF16)
    kv_out[:, :HD] = turn(mixed[:, HD : 2 * HD], cos[...], sin[...]).astype(BF16)
    kv_out[:, HD:] = mixed[:, 2 * HD :].astype(BF16)


def project_qkv(n1, w, bias, cos, sin):
    rows, depth = n1.shape
    heads = bias.shape[0]
    return pl.pallas_call(
        qkv_body,
        grid=(heads,),
        in_specs=[
            fixed((rows, depth)),
            pl.BlockSpec((depth, 3 * HD), lambda h: (0, h)),
            pl.BlockSpec((1, 1, 3 * HD), lambda h: (h, 0, 0)),
            fixed((rows, HD)),
            fixed((rows, HD)),
        ],
        out_specs=[
            pl.BlockSpec((rows, HD), lambda h: (0, h)),
            pl.BlockSpec((rows, 2 * HD), lambda h: (0, h)),
        ],
        out_shape=[
            jax.ShapeDtypeStruct((rows, heads * HD), BF16),
            jax.ShapeDtypeStruct((rows, heads * 2 * HD), BF16),
        ],
        compiler_params=params(),
        cost_estimate=cost(2 * rows * depth * heads * 3 * HD, 4 * rows * depth),
        name="project_qkv",
    )(n1, w, bias[:, None, :], cos, sin)


def first_of(place, ends, count):
    start = jnp.zeros_like(place)
    for n in range(count):
        start = jnp.where(place >= ends[n], ends[n], start)
    return start


def pair_visible(q_start, k_start, size, ends, count):
    begin = jnp.int32(0)
    for n in range(count):
        begin = jnp.where(q_start >= ends[n], ends[n], begin)
    return (k_start <= q_start + size - 1) & (k_start + size - 1 >= begin)


def allowed_mask(q_start, k_start, size, ends, count):
    q_place = q_start + lax.broadcasted_iota(jnp.int32, (size, 1), 0)
    k_place = k_start + lax.broadcasted_iota(jnp.int32, (1, size), 1)
    return (k_place <= q_place) & (k_place >= first_of(q_place, ends, count))


def attend_body(dims, meta, q, kv_own, kv_rem, o_out, exact_out, lse_out, top, main, extra):
    size, blocks, parts, count, pair = dims
    scale = HD ** (-0.5) * LOG2E
    j = pl.program_id(1)
    part = meta[count]
    span = size * parts
    ones = jnp.ones((size, HD), BF16)
    q_start = j * span + part * size
    top[...] = jnp.full_like(top, LOW)
    main[...] = jnp.zeros_like(main)
    extra[...] = jnp.zeros_like(extra)
    q_place = q_start + lax.broadcasted_iota(jnp.int32, (size, 1), 0)
    begin = first_of(q_place, meta, count)
    for shift in range(parts):
        owner = lax.rem(part + shift, parts)

        @pl.loop(0, j + 1)
        def _(jj):
            k_start = jj * span + owner * size

            @pl.when(pair_visible(q_start, k_start, size, meta, count))
            def _():
                if shift == 0:
                    there, kv = pl.ds(jj * size, size), kv_own
                else:
                    there, kv = pl.ds(((shift - 1) * blocks + jj) * size, size), kv_rem
                k_place = k_start + lax.broadcasted_iota(jnp.int32, (1, size), 1)
                allowed = (k_place <= q_place) & (k_place >= begin)
                for u in range(pair):
                    keys = kv[there, 2 * u * HD : (2 * u + 1) * HD]
                    values = kv[there, (2 * u + 1) * HD : (2 * u + 2) * HD]
                    s = dot(q[:, u * HD : (u + 1) * HD], keys, ((1,), (1,))) * scale
                    s = jnp.where(allowed, s, NEG)
                    old = top[u]
                    new = jnp.maximum(old, jnp.max(s, axis=1, keepdims=True))
                    p = jnp.exp2(s - new[:, :1])
                    fade = jnp.exp2(old - new)
                    fade = jnp.concatenate([fade, fade], axis=1)
                    coarse = p.astype(BF16)
                    fine = (p - coarse.astype(F32)).astype(BF16)
                    values = jnp.concatenate([values, ones], axis=1)
                    main[u] = main[u] * fade + dot(coarse, values)
                    extra[u] = extra[u] * fade + dot(fine, values)
                    top[u] = new

    for u in range(pair):
        here = slice(u * HD, (u + 1) * HD)
        exact = main[u] + extra[u]
        share = 1.0 / exact[:, HD:]
        o_out[:, here] = (main[u, :, :HD] * share).astype(BF16)
        exact_out[:, here] = exact[:, :HD] * share
        lse_out[:, here] = top[u] + jnp.log2(exact[:, HD:])


def attend(meta, q, kv_own, kv_rem, size, parts, count):
    rows, width = q.shape
    heads, blocks = width // HD, rows // size
    pair = next(n for n in (PAIR, 2, 1) if heads % n == 0)
    block = pl.BlockSpec((size, pair * HD), lambda h, j, *_: (j, h))
    return pl.pallas_call(
        functools.partial(attend_body, (size, blocks, parts, count, pair)),
        grid_spec=pltpu.PrefetchScalarGridSpec(
            num_scalar_prefetch=1,
            grid=(heads // pair, blocks),
            in_specs=[
                block,
                pl.BlockSpec((rows, 2 * pair * HD), lambda h, j, *_: (0, h)),
                pl.BlockSpec((rows * (parts - 1), 2 * pair * HD), lambda h, j, *_: (0, h)),
            ],
            out_specs=[block, block, block],
            scratch_shapes=[
                pltpu.VMEM((pair, size, HD), F32),
                pltpu.VMEM((pair, size, 2 * HD), F32),
                pltpu.VMEM((pair, size, 2 * HD), F32),
            ],
        ),
        out_shape=[
            jax.ShapeDtypeStruct((rows, width), BF16),
            jax.ShapeDtypeStruct((rows, width), F32),
            jax.ShapeDtypeStruct((rows, width), F32),
        ],
        compiler_params=params(2),
        cost_estimate=cost(12 * rows * rows * width, 30 * rows * width),
        name="attend",
    )(meta, q, kv_own, kv_rem)


def attend_back_body(
    dims, meta, q, kv_own, kv_rem, d_o, exact, lse, cos, sin, dq_out, own_out, rem_out, dq_sum, kv_sum
):
    size, blocks, parts, count = dims
    scale = HD ** (-0.5)
    part = meta[count]
    span = size * parts
    kv_sum[...] = jnp.zeros_like(kv_sum)

    @pl.loop(0, blocks)
    def _(j):
        q_start = j * span + part * size
        here = pl.ds(j * size, size)
        q_piece, do_piece = q[here, :], d_o[here, :]
        delta = jnp.sum(do_piece.astype(F32) * exact[here, :], axis=1, keepdims=True)
        level = lse[here, :][:, :1]
        dq_sum[...] = jnp.zeros_like(dq_sum)
        for shift in range(parts):
            owner = lax.rem(part + shift, parts)

            @pl.loop(0, j + 1)
            def _(jj):
                k_start = jj * span + owner * size

                @pl.when(pair_visible(q_start, k_start, size, meta, count))
                def _():
                    if shift == 0:
                        piece = kv_own[pl.ds(jj * size, size), :]
                    else:
                        piece = kv_rem[pl.ds(((shift - 1) * blocks + jj) * size, size), :]
                    there = pl.ds((shift * blocks + jj) * size, size)
                    allowed = allowed_mask(q_start, k_start, size, meta, count)
                    s = dot(q_piece, piece[:, :HD], ((1,), (1,))) * (scale * LOG2E)
                    p = jnp.where(allowed, jnp.exp2(s - level), 0.0)
                    dp = dot(do_piece, piece[:, HD:], ((1,), (1,)))
                    ds = (p * (dp - delta)).astype(BF16)
                    dq_sum[...] += dot(ds, piece[:, :HD])
                    kv_sum[there, :HD] += dot(ds, q_piece, ((0,), (0,)))
                    kv_sum[there, HD:] += dot(p.astype(BF16), do_piece, ((0,), (0,)))

        dq_out[here, :] = turn(dq_sum[...] * scale, cos[here, :], -sin[here, :]).astype(BF16)

    rows = blocks * size
    own_out[:, :HD] = kv_sum[:rows, :HD] * scale
    own_out[:, HD:] = kv_sum[:rows, HD:]
    rem_out[:, :HD] = (kv_sum[rows:, :HD] * scale).astype(BF16)
    rem_out[:, HD:] = kv_sum[rows:, HD:].astype(BF16)


def attend_back(meta, q, kv_own, kv_rem, d_o, exact, lse, cos, sin, size, parts, count):
    rows, width = q.shape
    heads, blocks = width // HD, rows // size
    narrow = pl.BlockSpec((rows, HD), lambda h, *_: (0, h))
    wide = pl.BlockSpec((rows, 2 * HD), lambda h, *_: (0, h))
    rest = pl.BlockSpec((rows * (parts - 1), 2 * HD), lambda h, *_: (0, h))
    return pl.pallas_call(
        functools.partial(attend_back_body, (size, blocks, parts, count)),
        grid_spec=pltpu.PrefetchScalarGridSpec(
            num_scalar_prefetch=1,
            grid=(heads,),
            in_specs=[narrow, wide, rest, narrow, narrow, narrow, fixed((rows, HD)), fixed((rows, HD))],
            out_specs=[narrow, wide, rest],
            scratch_shapes=[
                pltpu.VMEM((size, HD), F32),
                pltpu.VMEM((rows * parts, 2 * HD), F32),
            ],
        ),
        out_shape=[
            jax.ShapeDtypeStruct((rows, width), BF16),
            jax.ShapeDtypeStruct((rows, 2 * width), F32),
            jax.ShapeDtypeStruct((rows * (parts - 1), 2 * width), BF16),
        ],
        compiler_params=params(),
        cost_estimate=cost(20 * rows * rows * width, 40 * rows * width),
        name="attend_back",
    )(meta, q, kv_own, kv_rem, d_o, exact, lse, cos, sin)


def mix_body(arrived, dq, own, *refs):
    got, (cos, sin, out, bias_out) = refs[:arrived], refs[arrived:]
    total = own[...]
    for piece in got:
        total = total + piece[...].astype(F32)
    out[:, :HD] = dq[...]
    out[:, HD : 2 * HD] = turn(total[:, :HD], cos[...], -sin[...]).astype(BF16)
    out[:, 2 * HD :] = total[:, HD:].astype(BF16)
    bias_out[0] = jnp.sum(out[...].astype(F32), axis=0, keepdims=True)


def mix_back(dq, own, got, cos, sin):
    rows, width = dq.shape
    heads = width // HD
    wide = pl.BlockSpec((rows, 2 * HD), lambda h: (0, h))
    return pl.pallas_call(
        functools.partial(mix_body, len(got)),
        grid=(heads,),
        in_specs=[pl.BlockSpec((rows, HD), lambda h: (0, h)), wide]
        + [wide] * len(got)
        + [fixed((rows, HD)), fixed((rows, HD))],
        out_specs=[
            pl.BlockSpec((rows, 3 * HD), lambda h: (0, h)),
            pl.BlockSpec((1, 1, 3 * HD), lambda h: (h, 0, 0)),
        ],
        out_shape=[
            jax.ShapeDtypeStruct((rows, heads * 3 * HD), BF16),
            jax.ShapeDtypeStruct((heads, 1, 3 * HD), F32),
        ],
        compiler_params=params(),
        cost_estimate=cost(rows * width * 20, rows * width * 20),
        name="mix_back",
    )(dq, own, *got, cos, sin)


def plan_tiles(route_rows, weight_rows, block):
    rows, top = route_rows.shape
    blocks = rows // block
    per_tile = TM // PIECE
    room = (top * block + E * (PIECE - 1)) // PIECE
    number = (top * rows + E * blocks * (PIECE - 1) + E * TM) // TM
    experts = jnp.arange(E, dtype=jnp.int32)
    steps = jnp.arange(blocks, dtype=jnp.int32)
    match = route_rows[:, :, None] == experts
    spread = jnp.any(match, axis=1).T.reshape(E, blocks, block)
    order = jnp.arange(block, dtype=jnp.int32)
    before = (order[:, None] < order[None, :]).astype(BF16)
    rank = jnp.einsum("ebt,tu->ebu", spread.astype(BF16), before, preferred_element_type=F32)
    held = (jnp.sum(spread.astype(jnp.int32), axis=2) + PIECE - 1) // PIECE
    lower = (experts[:, None] < experts[None, :]).astype(jnp.int32)
    start = jnp.sum(lower[:, :, None] * held[:, None, :], axis=0)
    ahead = jnp.sum(
        jnp.where(steps[:, None] < steps[None, :], held[:, :, None], 0), axis=1
    )
    load = jnp.sum(held, axis=1)
    tiles = jnp.maximum((load + per_tile - 1) // per_tile, 1)
    begin = jnp.sum(lower * tiles[:, None], axis=0)
    spot = (rank.astype(jnp.int32) + start[:, :, None] * PIECE).reshape(E, rows).T
    spot = jnp.sum(jnp.where(match, spot[:, None, :], 0), axis=2)
    piece = jnp.arange(room, dtype=jnp.int32)
    inside = (piece[None, None, :] >= start[:, :, None]) & (
        piece[None, None, :] < (start + held)[:, :, None]
    )
    where_to = (begin[:, None] * per_tile + ahead - start)[:, :, None] + piece[None, None, :]
    where_to = jnp.sum(jnp.where(inside, where_to, 0), axis=0)
    halves = []
    for half in range(2):
        low, high = half * E // 2, (half + 1) * E // 2
        room_of = (top * rows + (high - low) * (blocks * (PIECE - 1) + TM)) // TM
        turn_in = jnp.arange(room_of, dtype=jnp.int32)
        from_tile = jnp.sum(tiles[:low])
        total = jnp.sum(tiles[low:high])
        place = from_tile + jnp.minimum(turn_in, total - 1)
        expert = jnp.sum((place[:, None] >= (begin + tiles)[None, :]).astype(jnp.int32), axis=1)
        pick = (expert[:, None] == experts[None, :]).astype(jnp.int32)
        turn_of = place - jnp.sum(pick * begin[None, :], axis=1)
        active = turn_in < total
        last = active & (turn_of == jnp.sum(pick * tiles[None, :], axis=1) - 1)
        limit = jnp.sum(pick * load[None, :], axis=1) * PIECE - turn_of * TM
        inner = turn_of[:, None] * per_tile + jnp.arange(per_tile, dtype=jnp.int32)[None, :]
        ahead_of = jnp.sum(pick[:, :, None] * ahead[None], axis=1)[:, None, :]
        held_of = jnp.sum(pick[:, :, None] * held[None], axis=1)[:, None, :]
        start_of = jnp.sum(pick[:, :, None] * start[None], axis=1)[:, None, :]
        inner = inner[:, :, None]
        inside = (inner >= ahead_of) & (inner < ahead_of + held_of)
        source = inner - ahead_of + start_of + (steps * room)[None, None, :]
        source = jnp.sum(jnp.where(inside, source, 0), axis=2)
        meta = jnp.stack(
            [
                expert,
                place,
                active.astype(jnp.int32),
                (active & (turn_of == 0)).astype(jnp.int32),
                last.astype(jnp.int32),
                limit,
            ]
        )
        halves.append((meta, source))
    spot = spot.reshape(blocks, block, top)
    weight = weight_rows.reshape(blocks, block, top)
    return dict(
        halves=halves,
        number=number,
        get=where_to,
        room=room,
        column=spot,
        line=jnp.swapaxes(spot, 1, 2),
        weight=weight,
        line_weight=jnp.swapaxes(weight, 1, 2),
    )


def send_out_body(dims, line, *refs):
    top, chunk, scaled = dims
    weight = refs[0] if scaled else None
    values, out, held = refs[-3:]
    rows, block = out.shape[1], values.shape[1]
    held[...] = values[0]

    @pl.loop(0, rows // chunk)
    def _(c):
        ids = lax.broadcasted_iota(jnp.int32, (chunk, block), 0) + c * chunk
        chosen = jnp.zeros((chunk, block), F32)
        level = jnp.zeros((chunk, block), F32)
        for r in range(top):
            hit = ids == line[0, r : r + 1, :]
            chosen = jnp.where(hit, 1.0, chosen)
            if scaled:
                level = jnp.where(hit, weight[0, r : r + 1, :], level)
        value = dot(chosen.astype(BF16), held[...])
        if scaled:
            value = value * jnp.sum(level, axis=1, keepdims=True)
        out[0, pl.ds(pl.multiple_of(c * chunk, chunk), chunk), :] = value.astype(BF16)


def send_out(plan, values, scaled):
    blocks, block, depth = values.shape
    top = plan["column"].shape[2]
    rows = plan["room"] * PIECE
    chunk = rows
    line = pl.BlockSpec((1, top, block), lambda b: (b, 0, 0))
    extra = [plan["line_weight"]] if scaled else []
    return pl.pallas_call(
        functools.partial(send_out_body, (top, chunk, scaled)),
        grid=(blocks,),
        in_specs=[line] * (1 + len(extra)) + [pl.BlockSpec((1, block, depth), lambda b: (b, 0, 0))],
        out_specs=pl.BlockSpec((1, rows, depth), lambda b: (b, 0, 0)),
        scratch_shapes=[pltpu.VMEM((block, depth), BF16)],
        out_shape=jax.ShapeDtypeStruct((blocks, rows, depth), BF16),
        compiler_params=params(),
        cost_estimate=cost(2 * blocks * rows * block * depth, 4 * blocks * rows * depth),
        name="send_out",
    )(plan["line"], *extra, values).reshape(blocks * rows, depth)


def bring_back_body(dims, get, column, *refs):
    blocks, top, room, weighted = dims
    weight = refs[0] if weighted else None
    packed, out, buf, sem = refs[-4:]
    b = pl.program_id(0)
    slot = lax.rem(b, 2)
    rows, block = buf.shape[1], out.shape[1]

    def fetch(which, into):
        @pl.loop(0, room)
        def _(i):
            pltpu.make_async_copy(
                packed.at[pl.ds(pl.multiple_of(get[which, i] * PIECE, PIECE), PIECE)],
                buf.at[into, pl.ds(pl.multiple_of(i * PIECE, PIECE), PIECE)],
                sem.at[into],
            ).start()

    @pl.when(b == 0)
    def _():
        fetch(b, slot)

    @pl.when(b < blocks - 1)
    def _():
        fetch(b + 1, 1 - slot)

    ids = lax.broadcasted_iota(jnp.int32, (block, rows), 1)
    chosen = jnp.zeros((block, rows), F32)
    for r in range(top):
        level = weight[0, :, r : r + 1] if weighted else 1.0
        chosen = jnp.where(ids == column[0, :, r : r + 1], level, chosen)
    pltpu.make_async_copy(packed.at[pl.ds(0, rows)], buf.at[slot], sem.at[slot]).wait()
    out[0] = dot(chosen.astype(BF16), buf[slot]).astype(BF16)


def bring_back(plan, packed, block, weighted):
    blocks, room = plan["get"].shape
    top = plan["column"].shape[2]
    depth = packed.shape[1]
    rows = room * PIECE
    column = pl.BlockSpec((1, block, top), lambda b, *_: (b, 0, 0))
    extra = [plan["weight"]] if weighted else []
    return pl.pallas_call(
        functools.partial(bring_back_body, (blocks, top, room, weighted)),
        grid_spec=pltpu.PrefetchScalarGridSpec(
            num_scalar_prefetch=1,
            grid=(blocks,),
            in_specs=[column] * (1 + len(extra)) + [pl.BlockSpec(memory_space=pl.ANY)],
            out_specs=pl.BlockSpec((1, block, depth), lambda b, *_: (b, 0, 0)),
            scratch_shapes=[pltpu.VMEM((2, rows, depth), BF16), pltpu.SemaphoreType.DMA((2,))],
        ),
        out_shape=jax.ShapeDtypeStruct((blocks, block, depth), BF16),
        compiler_params=params(),
        cost_estimate=cost(2 * blocks * rows * block * depth, 4 * blocks * rows * depth),
        name="bring_back",
    )(plan["get"], plan["column"], *extra, packed)


def experts_body(dims, meta, source, spot, x, d, gu_own, gu_rem, down_own, down_rem, *refs):
    cut, number, hidden, later = dims
    got, refs = (refs[:4], refs[6:]) if later else ((), refs)
    out, dx = refs[:2]
    results = refs[2:6]
    xs, ds, dgu = refs[6:9]
    totals, sem = refs[9:13], refs[13]
    i = pl.program_id(0)
    slot = lax.rem(i, 2)
    rows, cols = ((0,), (0,)), ((1,), (1,))

    def fetch(which, into):
        @pl.loop(0, TM // PIECE)
        def _(n):
            there = pl.ds(pl.multiple_of(source[which, n] * PIECE, PIECE), PIECE)
            here = pl.ds(pl.multiple_of(n * PIECE, PIECE), PIECE)
            pltpu.make_async_copy(x.at[there], xs.at[into, here], sem.at[0, into]).start()
            pltpu.make_async_copy(d.at[there], ds.at[into, here], sem.at[1, into]).start()

    @pl.when(i == 0)
    def _():
        fetch(i, slot)

    @pl.when((i < number - 1) & (meta[2, jnp.minimum(i + 1, number - 1)] == 1))
    def _():
        fetch(i + 1, 1 - slot)

    @pl.when(meta[3, i] == 1)
    def _():
        for total in totals:
            total[...] = jnp.zeros_like(total)

    @pl.when(meta[2, i] == 1)
    def _():
        pltpu.make_async_copy(x.at[pl.ds(0, TM)], xs.at[slot], sem.at[0, slot]).wait()
        pltpu.make_async_copy(d.at[pl.ds(0, TM)], ds.at[slot], sem.at[1, slot]).wait()
        limit = meta[5, i]

        @pl.when(limit < TM)
        def _():
            inside = lax.broadcasted_iota(jnp.int32, xs.shape[1:], 0) < limit
            for ref in (xs, ds):
                ref[slot] = jnp.where(inside, ref[slot], jnp.zeros(xs.shape[1:], BF16))

        x_own, x_rem = xs[slot, :, :cut], xs[slot, :, cut:]
        d_own, d_rem = ds[slot, :, :cut], ds[slot, :, cut:]
        both = dot(x_own, gu_own[0], cols) + dot(x_rem, gu_rem[0], cols)
        gate, up = both[:, :hidden], both[:, hidden:]
        d_hidden = dot(d_own, down_own[0], cols) + dot(d_rem, down_rem[0], cols)
        logistic = jax.nn.sigmoid(gate)
        act = gate * logistic
        h = (act * up).astype(BF16)
        dgu[:, :hidden] = (d_hidden * up * logistic * (1.0 + gate * (1.0 - logistic))).astype(BF16)
        dgu[:, hidden:] = (d_hidden * act).astype(BF16)
        out[:, :cut] = dot(h, down_own[0]).astype(BF16)
        out[:, cut:] = dot(h, down_rem[0]).astype(BF16)
        dx[:, :cut] = dot(dgu[...], gu_own[0]).astype(BF16)
        dx[:, cut:] = dot(dgu[...], gu_rem[0]).astype(BF16)
        totals[0][...] += dot(dgu[...], x_own, rows)
        totals[1][...] += dot(dgu[...], x_rem, rows)
        totals[2][...] += dot(h, d_own, rows)
        totals[3][...] += dot(h, d_rem, rows)

    @pl.when(meta[4, i] == 1)
    def _():
        for n, (total, to) in enumerate(zip(totals, results)):
            if later:
                to[0] = (total[...] + got[n][0].astype(F32)).astype(BF16)
            else:
                to[0] = total[...].astype(BF16)


def experts(plan, half, spot, x, d, weights, copies, got=(), filled=()):
    meta, source = plan["halves"][half]
    depth = x.shape[1]
    hidden, cut = weights[2].shape[1:]
    rest = depth - cut
    number = meta.shape[1]
    quarter = E // copies
    own_at = lambda i, meta, source, spot: (meta[0, i] ^ spot[1], 0, 0)
    rem_at = lambda i, meta, source, spot: (
        (((meta[0, i] ^ spot[1]) // quarter) ^ spot[0]) * quarter + meta[0, i] % quarter,
        0,
        0,
    )
    half_at = lambda i, meta, *_: (meta[0, i] - half * (E // 2), 0, 0)
    tile = pl.BlockSpec((TM, depth), lambda i, meta, *_: (meta[1, i], 0))
    shapes = [(2 * hidden, cut), (2 * hidden, rest), (hidden, cut), (hidden, rest)]
    anywhere = pl.BlockSpec(memory_space=pl.ANY)
    results = [pl.BlockSpec((1,) + s, half_at) for s in shapes]
    return pl.pallas_call(
        functools.partial(experts_body, (cut, number, hidden, half == 1)),
        grid_spec=pltpu.PrefetchScalarGridSpec(
            num_scalar_prefetch=3,
            grid=(number,),
            in_specs=[anywhere] * 2
            + [pl.BlockSpec((1,) + s, at) for s, at in zip(shapes, (own_at, rem_at) * 2)]
            + (results + [anywhere] * 2 if half else []),
            out_specs=[tile, tile] + results,
            scratch_shapes=[pltpu.VMEM((2, TM, depth), BF16)] * 2
            + [pltpu.VMEM((TM, 2 * hidden), BF16)]
            + [pltpu.VMEM(s, F32) for s in shapes]
            + [pltpu.SemaphoreType.DMA((2, 2))],
        ),
        out_shape=[jax.ShapeDtypeStruct((plan["number"] * TM, depth), BF16)] * 2
        + [jax.ShapeDtypeStruct((E // 2,) + s, BF16) for s in shapes],
        input_output_aliases={13: 0, 14: 1} if half else {},
        compiler_params=params(),
        cost_estimate=cost(9 * plan["number"] * TM * depth * hidden, 6 * E * depth * hidden + number * TM * depth * 4),
        name=("experts_first", "experts_second")[half],
    )(meta, source, spot, x, d, *weights, *got, *filled)


def from_ahead(values, shift):
    n = lax.axis_size("gy")
    return lax.ppermute(values, "gy", [(s, (s - shift) % n) for s in range(n)])


def across(values, bit):
    n = lax.axis_size("dp")
    return lax.ppermute(values, "dp", [(d, d ^ bit) for d in range(n)])


def bits():
    n, bit, out = lax.axis_size("dp"), 1, []
    while bit < n:
        out.append(bit)
        bit *= 2
    return out


def tie(values, *others):
    return lax.optimization_barrier((values, others))[0]


class Spread:
    def __init__(self, weights):
        self.weights = weights

    def cut(self):
        copies, me = lax.axis_size("dp"), lax.axis_index("dp")
        return [
            lax.dynamic_slice_in_dim(w, me * (w.shape[0] // copies), w.shape[0] // copies)
            for w, _ in self.weights
        ]

    def over_gy(self, pieces):
        parts = lax.axis_size("gy")
        out = []
        for piece, (_, axis) in zip(pieces, self.weights):
            got = [from_ahead(piece, k) for k in range(1, parts)]
            out.append({0: got[0] if len(got) == 1 else jnp.concatenate(got, axis=axis)})
        return out

    def over_dp(self, held, level):
        bit = list(reversed(bits()))[level]
        return [h | {key | bit: across(part, bit) for key, part in h.items()} for h in held]


def keyed(held):
    return jnp.concatenate([held[key] for key in range(len(held))], axis=0)


def whole(weight, axis, held):
    me = lax.axis_index("dp")
    stack = [held[key] for key in range(len(held))]
    for bit in bits():
        swap = (me & bit) != 0
        stack = [jnp.where(swap, stack[n ^ bit], stack[n]) for n in range(len(stack))]
    return jnp.concatenate([weight, jnp.concatenate(stack, axis=0)], axis=axis)


def to_rows(values):
    parts, me = lax.axis_size("gy"), lax.axis_index("gy")
    share = values.shape[0] // parts
    take = lambda k: lax.dynamic_slice_in_dim(values, ((me - k + parts) % parts) * share, share)
    return jnp.concatenate(
        [take(0)] + [from_ahead(take(k), k) for k in range(1, parts)], axis=1
    )


def to_columns(values, kind):
    parts, me = lax.axis_size("gy"), lax.axis_index("gy")
    width = values.shape[1] // parts
    blocks = []
    for k in range(parts):
        block = values[:, k * width : (k + 1) * width]
        blocks.append((from_ahead(block.astype(BF16), parts - k) if k else block).astype(kind))
    return jnp.concatenate(in_order([blocks[(parts - k) % parts] for k in range(parts)], me), axis=0)


def in_order(blocks, me):
    n = len(blocks)
    out = []
    for place in range(n):
        block = blocks[place]
        for k in range(n):
            block = jnp.where(me == (place - k) % n, blocks[k], block)
        out.append(block)
    return out


class Reduce:
    def __init__(self):
        self.side = lax.axis_index("dp") & 1

    def pick(self, values, side):
        half = values.shape[0] // 2
        return lax.dynamic_slice_in_dim(values, side * half, half)

    def near(self, grads):
        sums = []
        for grad in grads:
            sums.append([])
            for v in grad:
                got = across(self.pick(v, 1 - self.side), 1)
                sums[-1].append((self.pick(v, self.side).astype(F32) + got.astype(F32)).astype(BF16))
        return sums

    def over_gy(self, sums):
        parts = lax.axis_size("gy")
        out = []
        for own, *rest in sums:
            total = own.astype(F32)
            for k, piece in enumerate(rest, start=1):
                total = total + from_ahead(piece, parts - k).astype(F32)
            out.append(total.astype(BF16))
        return out

    def over_dp(self, sums):
        for bit in bits()[1:]:
            sums = [(t.astype(F32) + across(t, bit).astype(F32)).astype(BF16) for t in sums]
        return sums

    def finish(self, sums):
        out = []
        for total in sums:
            other = across(total, 1)
            first = jnp.where(self.side == 0, total, other).astype(F32)
            second = jnp.where(self.side == 0, other, total).astype(F32)
            out.append(jnp.concatenate([first, second], axis=0))
        return out


def split_blocks(values, parts, axis):
    width = values.shape[axis] // parts
    return [lax.slice_in_dim(values, k * width, (k + 1) * width, axis=axis) for k in range(parts)]


def gather_rows(values):
    return lax.all_gather(values, "gx", axis=0, tiled=True)


def sum_rows(values):
    return lax.psum_scatter(values, "gx", scatter_dimension=0, tiled=True)


def local(
    stream_in, lengths, routes, route_weights, norm_attn, w_qkv, qkv_bias, w_out, norm_ffn, w_gate, w_up,
    w_down, shared_gate, shared_up, shared_down, shared_router, cotangent
):
    parts, gy = lax.axis_size("gy"), lax.axis_index("gy")
    groups, gx = lax.axis_size("gx"), lax.axis_index("gx")
    dp = lax.axis_index("dp")
    held, width = stream_in.shape
    depth = width * parts
    size = held // parts
    rows = size * groups
    heads = qkv_bias.shape[0]
    count = lengths.shape[0]

    numbers = jnp.arange(count)
    ends = jnp.sum(jnp.where(numbers[:, None] <= numbers[None, :], lengths[:, None], 0), axis=0)
    ends = ends.astype(jnp.int32)
    row = jnp.arange(rows, dtype=jnp.int32)
    place = (row // size) * held + gy * size + row % size
    begin = jnp.zeros_like(place)
    for n in range(count):
        begin = jnp.where(place >= ends[n], ends[n], begin)
    mine = gx * held + gy * size + jnp.arange(size, dtype=jnp.int32)
    valid = (mine < ends[count - 1]).astype(F32)[:, None]
    half = HD // 2
    angles = (place - begin).astype(F32)[:, None] * (
        THETA ** (-jnp.arange(half, dtype=F32) * 2.0 / HD)
    )[None, :]
    cos, sin = jnp.cos(angles), jnp.sin(angles)
    cos = jnp.concatenate([cos, cos], axis=1)
    sin = jnp.concatenate([-sin, sin], axis=1)
    span = jnp.concatenate([ends, gy[None].astype(jnp.int32)])

    narrow = jnp.concatenate([norm_attn[None], norm_ffn[None], shared_router[None]])
    stream_rows, dy_rows = to_rows(stream_in), to_rows(cotangent)
    narrow = jnp.concatenate([narrow] + [from_ahead(narrow, k) for k in range(1, parts)], axis=1)
    gain_attn, gain_ffn, router = (narrow[n].astype(F32)[None, :] for n in range(3))
    flat_qkv = w_qkv.reshape(width, heads * 3 * HD)
    lead = Spread([(flat_qkv, 0), (w_out, 1)])
    gate_t, up_t = jnp.swapaxes(w_gate, 1, 2), jnp.swapaxes(w_up, 1, 2)
    early = Spread([(shared_gate, 0), (shared_up, 0), (shared_down, 1), (gate_t, 2)])
    late = [Spread([(up_t, 2)]), Spread([(w_down, 2)])]

    stream = stream_rows.astype(F32)
    inv_attn = lax.rsqrt(jnp.mean(stream * stream, axis=1, keepdims=True) + EPS)
    unit_attn = stream * inv_attn
    n1_part = (unit_attn * gain_attn).astype(BF16)
    lead_held = lead.over_gy(tie(lead.cut(), stream_rows))
    masked = dy_rows.astype(F32) * valid
    dy_part = masked.astype(BF16)
    early_held = early.over_gy(tie(early.cut(), dy_rows))
    n1 = gather_rows(n1_part)
    lead_held = lead.over_dp(lead_held, 0)
    lead_held = lead.over_dp(lead_held, 1)
    qkv_all = whole(flat_qkv, 0, lead_held[0])
    out_all = whole(w_out, 1, lead_held[1])
    block = 256 if rows % 256 == 0 else 128
    shape = (rows // block, block, depth)
    take = lambda v: lax.dynamic_index_in_dim(
        v.reshape(groups, parts, size, v.shape[1]), gy, 1, keepdims=False
    ).reshape(rows, v.shape[1])
    flip = (1 - (dp & 1)) * (E // 2)
    plan = plan_tiles(take(routes) ^ flip, take(route_weights), block)
    spot = jnp.stack([dp, flip]).astype(jnp.int32)
    tables = {name: table for name, table in plan.items() if name not in ("room", "number")}
    n1, dy_part, qkv_all, out_all, early_held[2:], tables = lax.optimization_barrier(
        (n1, dy_part, qkv_all, out_all, early_held[2:], tables)
    )
    plan |= tables
    dy = gather_rows(dy_part)

    q, kv = project_qkv(n1, qkv_all, qkv_bias, cos, sin)
    kv, early_held = lax.optimization_barrier((kv, early_held))
    kv_rest = [from_ahead(kv, k) for k in range(1, parts)]
    kv_rest = kv_rest[0] if parts == 2 else jnp.concatenate(kv_rest, axis=0)
    shared_held, gate_held = early_held[:3], early_held[3:]
    gate_held = early.over_dp(gate_held, 0)
    kv_rest, gate_held = lax.optimization_barrier((kv_rest, gate_held))
    shared_held = early.over_dp(shared_held, 0)
    up_held = late[0].over_gy(tie(late[0].cut(), kv_rest))
    o, o_exact, level = attend(span, q, kv, kv_rest, size, parts, count)
    o, shared_held = lax.optimization_barrier((o, shared_held))
    attn_part = dot(o, out_all).astype(BF16)
    attn_part, dy, up_held = lax.optimization_barrier((attn_part, dy, up_held))
    attn = sum_rows(attn_part).astype(F32)
    down_held = late[1].over_gy(tie(late[1].cut(), attn_part))
    shared_held = early.over_dp(shared_held, 1)
    gate_held = early.over_dp(gate_held, 1)
    up_held = late[0].over_dp(up_held, 0)

    d_slots = send_out(plan, dy.reshape(shape), True)
    sg_all = whole(shared_gate, 0, shared_held[0])
    su_all = whole(shared_up, 0, shared_held[1])
    sd_all = whole(shared_down, 1, shared_held[2])
    cols, both = ((1,), (1,)), ((0,), (0,))
    d_s_hidden = dot(dy, sd_all, cols)

    middle = stream + attn
    inv_ffn = lax.rsqrt(jnp.mean(middle * middle, axis=1, keepdims=True) + EPS)
    unit_ffn = middle * inv_ffn
    n2_part = (unit_ffn * gain_ffn).astype(BF16)
    n2_part, up_held, down_held, d_slots, d_s_hidden = lax.optimization_barrier(
        (n2_part, up_held, down_held, d_slots, d_s_hidden)
    )
    n2 = gather_rows(n2_part)
    up_held = late[0].over_dp(up_held, 1)
    down_held = late[1].over_dp(down_held, 0)
    down_held = late[1].over_dp(down_held, 1)
    copies = lax.axis_size("dp")
    weights = [
        jnp.concatenate([gate_t, up_t], axis=1),
        jnp.concatenate(
            [jnp.concatenate([gate_held[0][key], up_held[0][key]], axis=1) for key in range(copies)], axis=0
        ),
        w_down,
        keyed(down_held[0]),
    ]

    n2, weights = lax.optimization_barrier((n2, weights))
    x_slots = send_out(plan, n2.reshape(shape), False)
    out_slots, dx_slots, *given = experts(plan, 0, spot, x_slots, d_slots, weights, copies)

    n2_s = tie(n2, given)
    got = [across(v, 1) for v in given]
    logit = jnp.sum(n2_s.astype(F32) * router, axis=1, keepdims=True)
    mixer = jax.nn.sigmoid(logit)
    sgate, sup = dot(n2_s, sg_all), dot(n2_s, su_all)
    s_logistic = jax.nn.sigmoid(sgate)
    s_act = sgate * s_logistic
    s_hidden = (mixer * s_act * sup).astype(BF16)
    d_sgate = (d_s_hidden * mixer * sup * s_logistic * (1.0 + sgate * (1.0 - s_logistic))).astype(BF16)
    d_sup = (d_s_hidden * mixer * s_act).astype(BF16)
    d_logit = jnp.sum(d_s_hidden * s_act * sup, axis=1, keepdims=True) * mixer * (1.0 - mixer)
    pieces = [
        [dot(a, d_sgate, both).astype(BF16) for a in split_blocks(n2_s, parts, 1)],
        [dot(a, d_sup, both).astype(BF16) for a in split_blocks(n2_s, parts, 1)],
        [dot(s_hidden, a, both).astype(BF16) for a in split_blocks(dy, parts, 1)],
    ]
    reduce = Reduce()
    shared_sums = reduce.near(pieces)
    dn2_shared = (
        dot(d_sgate, sg_all, cols) + dot(d_sup, su_all, cols) + d_logit * router
    ).astype(BF16)

    x_slots, shared_sums, dn2_shared, got = lax.optimization_barrier(
        (x_slots, shared_sums, dn2_shared, got)
    )
    out_slots, dx_slots, *sums = experts(
        plan, 1, spot, x_slots, d_slots, weights, copies, got, (out_slots, dx_slots)
    )
    shared_sums = reduce.over_gy(shared_sums)
    dx_slots, out_slots, shared_sums, sums = lax.optimization_barrier(
        (dx_slots, out_slots, shared_sums, sums)
    )
    down_sums = [[sums[2]] + split_blocks(sums[3], parts - 1, 2)]
    cuts = (0, E // 4, 3 * E // 8, E // 2)
    gu_sums = [
        [[sums[0][low:high]] + split_blocks(sums[1][low:high], parts - 1, 2)]
        for low, high in zip(cuts, cuts[1:])
    ]
    dn2 = bring_back(plan, dx_slots, block, False)
    dn2 = (dn2.reshape(rows, depth).astype(F32) + dn2_shared.astype(F32)).astype(BF16)
    d_n2 = sum_rows(dn2).astype(F32)
    down_sums = reduce.over_gy(down_sums)
    shared_sums = reduce.over_dp(shared_sums)
    routed = bring_back(plan, tie(out_slots, dn2), block, True)
    branch_part = (routed.reshape(rows, depth).astype(F32) + dot(s_hidden, sd_all)).astype(BF16)
    router_part = jnp.sum(d_logit * n2_s.astype(F32), axis=0)

    gain_ffn_part = jnp.sum(d_n2 * unit_ffn, axis=0)
    scaled = d_n2 * gain_ffn
    d_middle = masked + inv_ffn * (
        scaled - unit_ffn * jnp.mean(scaled * unit_ffn, axis=1, keepdims=True)
    )

    d_mid_part = d_middle.astype(BF16)
    d_mid_part, down_sums, branch_part, shared_sums, gu_sums = lax.optimization_barrier(
        (d_mid_part, down_sums, branch_part, shared_sums, gu_sums)
    )
    d_mid = gather_rows(d_mid_part)
    gu_sums[0] = reduce.over_gy(gu_sums[0])
    down_sums = reduce.over_dp(down_sums)
    grad_sgate, grad_sup, grad_sdown = reduce.finish(shared_sums)
    d_mid, gu_sums, down_sums, branch_part = lax.optimization_barrier(
        (d_mid, gu_sums, down_sums, branch_part)
    )
    branch = sum_rows(branch_part).astype(F32)
    d_o = dot(d_mid, out_all, cols).astype(BF16)
    gu_sums[0] = reduce.over_dp(gu_sums[0])
    gu_sums[1] = reduce.over_gy(gu_sums[1])
    dq, dkv_own, dkv_rest = attend_back(
        span, q, kv, kv_rest, d_o, o_exact, level, cos, sin, size, parts, count
    )
    dkv_rest, gu_sums[1:] = lax.optimization_barrier((dkv_rest, gu_sums[1:]))
    out_sums = reduce.near([[dot(o, b, both).astype(BF16) for b in split_blocks(d_mid, parts, 1)]])
    got = [
        from_ahead(piece, parts - k)
        for k, piece in enumerate(split_blocks(dkv_rest, parts - 1, 0), start=1)
    ]
    [grad_down] = reduce.finish(down_sums)
    got, out_sums, gu_sums = lax.optimization_barrier((got, out_sums, gu_sums))
    gu_sums[1] = reduce.over_dp(gu_sums[1])
    gu_sums[2] = reduce.over_gy(gu_sums[2])
    d_mixed, bias_part = mix_back(dq, dkv_own, got, cos, sin)
    d_n1_part = dot(d_mixed, qkv_all, cols).astype(BF16)
    d_n1_part, d_mixed, branch = lax.optimization_barrier((d_n1_part, d_mixed, branch))
    d_n1 = sum_rows(d_n1_part).astype(F32)
    result = middle + branch
    qkv_sums = reduce.near([[dot(a, d_mixed, both).astype(BF16) for a in split_blocks(n1, parts, 1)]])
    attn_sums = qkv_sums + out_sums
    attn_sums, gu_sums[1:] = lax.optimization_barrier((attn_sums, gu_sums[1:]))
    gu_sums[2] = reduce.over_dp(gu_sums[2])
    attn_sums = reduce.over_gy(attn_sums)
    attn_sums, d_n1 = lax.optimization_barrier((attn_sums, d_n1))
    grad_w_qkv, grad_w_out = reduce.finish(reduce.over_dp(attn_sums))
    grad_w_qkv = grad_w_qkv.reshape(width, heads, 3 * HD)
    gain_attn_part = jnp.sum(d_n1 * unit_attn, axis=0)
    scaled = d_n1 * gain_attn
    grad_stream = d_middle + inv_attn * (
        scaled - unit_attn * jnp.mean(scaled * unit_attn, axis=1, keepdims=True)
    )

    sums = jnp.stack([gain_attn_part, gain_ffn_part, router_part])
    sums = lax.dynamic_slice_in_dim(
        jnp.concatenate([sums, sums], axis=1), ((parts - gy) % parts) * width, depth, axis=1
    )
    flat_bias = bias_part.reshape(-1)
    biases = lax.dynamic_update_slice_in_dim(
        jnp.zeros((groups * flat_bias.shape[0],), F32), flat_bias, gx * flat_bias.shape[0], 0
    )
    squares = jnp.stack(
        [jnp.sum(valid * v * v) for v in (middle, result, attn, branch)] + [jnp.sum(valid) * depth]
    )
    sums = lax.psum(jnp.concatenate([sums.reshape(-1), biases, squares]), ("dp", "gx", "gy"))
    vectors = lax.dynamic_slice_in_dim(sums[: 3 * depth].reshape(3, depth), gy * width, width, axis=1)
    bias_sum = lax.dynamic_slice_in_dim(sums[3 * depth : -5], gx * heads * 3 * HD, heads * 3 * HD)
    bias_sum = bias_sum.reshape(heads, 3 * HD)
    grad_columns = to_columns(grad_stream, F32)
    hidden = gate_t.shape[1]
    gu = [gu_sum for [gu_sum] in gu_sums]
    gu[2], grad_columns = lax.optimization_barrier((gu[2], grad_columns))
    gu_other = [across(v, 1) for v in gu]
    side = dp & 1
    grad_gate, grad_up = (
        jnp.swapaxes(
            jnp.concatenate(
                [jnp.where(side == 0, a[:, part], b[:, part]).astype(F32) for a, b in zip(gu, gu_other)]
                + [jnp.where(side == 0, b[:, part], a[:, part]).astype(F32) for a, b in zip(gu, gu_other)],
                axis=0,
            ),
            1,
            2,
        )
        for part in (slice(0, hidden), slice(hidden, 2 * hidden))
    )
    rms_stats = jnp.sqrt(sums[-5:-1] / sums[-1])
    return (
        to_columns(result, BF16),
        grad_columns,
        vectors[0],
        grad_w_qkv,
        bias_sum,
        grad_w_out,
        vectors[1],
        grad_gate,
        grad_up,
        grad_down,
        grad_sgate,
        grad_sup,
        grad_sdown,
        vectors[2],
        rms_stats,
    )


def solution(mesh):
    placed = (
        P(("dp", "gx"), "gy"),
        P("dp"),
        P("dp", None),
        P("dp", None),
        P("gy"),
        P("gy", "gx", None),
        P("gx", None),
        P("gx", "gy"),
        P("gy"),
        P(None, "gy", "gx"),
        P(None, "gy", "gx"),
        P(None, "gx", "gy"),
        P("gy", "gx"),
        P("gy", "gx"),
        P("gx", "gy"),
        P("gy"),
        P(("dp", "gx"), "gy"),
    )
    return jax.shard_map(
        local,
        mesh=mesh,
        in_specs=placed,
        out_specs=(
            P(("dp", "gx"), "gy"),
            P(("dp", "gx"), "gy"),
            P("gy"),
            P("gy", "gx", None),
            P("gx", None),
            P("gx", "gy"),
            P("gy"),
            P(None, "gy", "gx"),
            P(None, "gy", "gx"),
            P(None, "gx", "gy"),
            P("gy", "gx"),
            P("gy", "gx"),
            P("gx", "gy"),
            P("gy"),
            P(),
        ),
        check_vma=False,
    )
```
